512 devices in a mesh: row: 32 (over z, x), col: 16 (over y, core).
Axes of the slice: x: 4, y: 8, z: 8, core: 2. Of those that a mesh axis runs over, the one named last changes fastest.
Arguments:
- momentum: bfloat16 [4, 1536, 7168], P(None, 'row', 'col'), may hold values from -0.048339844 to 0.048339844
Outputs:
- orthogonal: bfloat16 [4, 1536, 7168], P(None, 'row', 'col')
The draws below stay inside these ranges and needn't reach their ends.
All inputs are finite; a program needn't handle non-finite values.
Results may differ from the reference program's by a relative error of at most 0.0054.
Values may be sent and summed in bfloat16 or wider, within the bound.
No kernel may reach another device: no remote copies, remote signals or barrier semaphores. Data moves between devices by JAX's collectives and lax.ppermute only.
A program may use at most 64 MiB of HBM per device.

```python
import math
import jax
import jax.numpy as jnp
from jax import lax

N = 7168
M = 1536
LAYERS = 4


def levels(stream_key, dims, split, low, largest):
    def one(axis_at, blocks):
        heights = jax.random.uniform(jax.random.fold_in(jax.random.fold_in(stream_key, 6), axis_at), (blocks,), jnp.float32, low / len(split), largest / len(split))
        return jnp.repeat(jnp.exp(heights), dims[axis_at] // blocks).reshape((-1,) + (1,) * (len(dims) - axis_at - 1))

    level = one(*split[0])
    for cut in split[1:]:
        level = level * one(*cut)
    return level


def gaussian(key, dims, width, bound, split=(), dtype=jnp.bfloat16):
    drawn = jax.random.normal(key, dims, jnp.float32) * width
    if len(split) > 0:
        drawn = levels(key, dims, split, -0.22, 0.18) * drawn
    return jnp.clip(drawn, min=-bound, max=bound).astype(dtype)


def setup_inputs(seed: int = 0) -> dict:
    splits = jax.random.split(jax.random.key(seed), 2)
    momentum = gaussian(splits[0], (LAYERS, M, N), (1.0 / (N ** 0.5 + M ** 0.5)), 0.048339844, ((1, 32), (2, 16)))
    return dict(momentum=momentum)


def reference(momentum):
    iterate = momentum.astype(jnp.float32)
    high = lax.Precision.HIGHEST
    gram = jnp.einsum('lin,ljn->lij', iterate, iterate, precision=high).astype(jnp.bfloat16)
    gram_f = gram.astype(jnp.float32)
    square = jnp.einsum('lik,lkj->lij', gram_f, gram_f, precision=high)
    poly = (-4.775 * gram_f + 2.0315 * square).astype(jnp.bfloat16)
    product = jnp.einsum('lik,lkn->lin', poly.astype(jnp.float32), iterate, precision=high)
    return (0.2 * math.sqrt(N) * (3.4445 * iterate + product)).astype(jnp.bfloat16)
```

```python
import math

import jax
import jax.numpy as jnp
from jax import lax
from jax.sharding import Mesh, PartitionSpec as P

F32 = jnp.float32
BF16 = jnp.bfloat16
A1, A3, A5 = 3.4445, -4.775, 2.0315
ZX = ("zq", "zh", "x")
HY = ("zh", "y")


def swap(array):
    return lax.ppermute(array, "core", [(0, 1), (1, 0)])


def exchange(array, axes):
    return lax.all_to_all(array, axes, 0, 0, tiled=True)


def tiles(panel):
    return panel.reshape(4, 48, 4, 384).transpose(0, 2, 1, 3).reshape(16, 48, 384)


def panel_of(tiled):
    return tiled.reshape(4, 4, 48, 384).transpose(0, 2, 1, 3).reshape(192, 1536)


def local(momentum):
    width = 7168
    zq, core = lax.axis_index("zq"), lax.axis_index("core")
    own, other = zq * 384 + core * 192, zq * 384 + (1 - core) * 192

    low = momentum[:, :, :256]
    high = jnp.pad(momentum[:, :, 256:], ((0, 0), (0, 0), (0, 64)))
    halves = jnp.stack([low, high])
    sent = jnp.broadcast_to(halves[None], (4, 2, 4, 48, 256)).reshape(32, 48, 256)
    m = exchange(sent, ZX).reshape(1536, 256)

    m_own = lax.dynamic_slice(m, (own, 0), (192, 256))
    m_other = lax.dynamic_slice(m, (other, 0), (192, 256))

    def gram(rows):
        return lax.dot_general(rows, m, (((1,), (1,)), ((), ())), preferred_element_type=F32)

    away = swap(tiles(gram(m_other).astype(BF16)))
    part = (tiles(gram(m_own)) + away.astype(F32)).astype(BF16)
    parts = exchange(part, HY)
    tile = jnp.sum(parts.astype(F32), axis=0).astype(BF16)
    gathered = exchange(jnp.broadcast_to(tile[None], (16, 48, 384)), HY)

    def partial(tiled, rows):
        g = panel_of(tiled)
        gm = jnp.dot(g, m, preferred_element_type=F32)
        w = (A3 * rows.astype(F32) + A5 * gm).astype(BF16)
        return lax.dot_general(g, w, (((0,), (0,)), ((), ())), preferred_element_type=F32)

    total = partial(gathered, m_own) + partial(swap(gathered), m_other)
    back = exchange(total.astype(BF16).reshape(32, 48, 256), ZX)
    summed = jnp.sum(back.reshape(4, 2, 4, 48, 256).astype(F32), axis=0)
    product = jnp.concatenate([summed[0], summed[1][:, :, :192]], axis=2)
    result = 0.2 * math.sqrt(width) * (A1 * momentum.astype(F32) + product)
    return result.astype(BF16)


def solution(mesh):
    split = Mesh(mesh.devices.reshape(4, 2, 4, 8, 2), ("zq", "zh", "x", "y", "core"))
    placed = P(None, ZX, ("y", "core"))
    return jax.shard_map(local, mesh=split, in_specs=(placed,), out_specs=placed, check_vma=False)
```

```python
import math

import jax
import jax.numpy as jnp
from jax import lax
from jax.experimental import pallas as pl
from jax.experimental.pallas import tpu as pltpu
from jax.sharding import Mesh, PartitionSpec as P

F32 = jnp.float32
BF16 = jnp.bfloat16
A1, A3, A5 = 3.4445, -4.775, 2.0315
ZX = ("zq", "zh", "x")
HY = ("zh", "y")
VMEM = pl.BlockSpec(memory_space=pltpu.VMEM)


def kernel_call(body, inputs, shape, dtype, flops):
    return pl.pallas_call(
        body,
        out_shape=jax.ShapeDtypeStruct(shape, dtype),
        in_specs=[VMEM] * len(inputs),
        out_specs=VMEM,
        cost_estimate=pl.CostEstimate(flops=flops, bytes_accessed=0, transcendentals=0),
        compiler_params=pltpu.CompilerParams(vmem_limit_bytes=40 * 2**20),
    )(*inputs)


def swap(array):
    return lax.ppermute(array, "core", [(0, 1), (1, 0)])


def exchange(array, axes):
    return lax.all_to_all(array, axes, 0, 0, tiled=True)


def first_block(other):
    core = lax.axis_index("core")
    return lax.axis_index("zq") * 8 + (1 - core if other else core) * 4


def pack_body(momentum, sent):
    for layer in range(4):
        low = momentum[layer, :, :256]
        high = jnp.concatenate([momentum[layer, :, 256:], jnp.zeros((48, 64), BF16)], axis=1)
        for quarter in range(4):
            sent[quarter * 8 + layer] = low
            sent[quarter * 8 + 4 + layer] = high


def gram_body(other):
    def body(m, out):
        rows = m[pl.ds(first_block(other), 4)].reshape(192, 256)
        for cg in range(4):
            columns = m[cg * 8 : cg * 8 + 8].reshape(384, 256)
            block = lax.dot_general(
                rows, columns, (((1,), (1,)), ((), ())), preferred_element_type=F32
            )
            for rg in range(4):
                out[rg * 4 + cg] = block[rg * 48 : rg * 48 + 48].astype(out.dtype)

    return body


def product_terms(m, tiles, other):
    panels = [jnp.concatenate([tiles[rg * 4 + cg] for rg in range(4)], axis=0) for cg in range(4)]
    gm = jnp.zeros((192, 256), F32)
    for cg in range(4):
        rows = m[cg * 8 : cg * 8 + 8].reshape(384, 256)
        gm = gm + jnp.dot(panels[cg], rows, preferred_element_type=F32)
    own = m[pl.ds(first_block(other), 4)].reshape(192, 256).astype(F32)
    w = (A3 * own + A5 * gm).astype(BF16)
    for cg in range(4):
        yield lax.dot_general(panels[cg], w, (((0,), (0,)), ((), ())), preferred_element_type=F32)


def product_body(m, tiles, out):
    for cg, piece in enumerate(product_terms(m, tiles, False)):
        out[cg * 8 : cg * 8 + 8] = piece.reshape(8, 48, 256)


def product_add_body(m, tiles, partial, out):
    for cg, piece in enumerate(product_terms(m, tiles, True)):
        block = slice(cg * 8, cg * 8 + 8)
        out[block] = (partial[block] + piece.reshape(8, 48, 256)).astype(BF16)


def local(momentum):
    width = 7168
    m = exchange(kernel_call(pack_body, [momentum], (32, 48, 256), BF16, 10**6), ZX)

    gram_flops = 2 * 192 * 1536 * 256
    away = swap(kernel_call(gram_body(True), [m], (16, 48, 384), BF16, gram_flops))
    own = kernel_call(gram_body(False), [m], (16, 48, 384), F32, gram_flops)
    part = (own + away.astype(F32)).astype(BF16)
    parts = exchange(part, HY)
    tile = jnp.sum(parts.astype(F32), axis=0).astype(BF16)
    gathered = exchange(jnp.broadcast_to(tile[None], (16, 48, 384)), HY)

    others = swap(gathered)
    partial = kernel_call(product_body, [m, gathered], (32, 48, 256), F32, 2 * gram_flops)
    total = kernel_call(
        product_add_body, [m, others, partial], (32, 48, 256), BF16, 2 * gram_flops
    )
    back = exchange(total, ZX)
    summed = jnp.sum(back.reshape(4, 2, 4, 48, 256).astype(F32), axis=0)
    product = jnp.concatenate([summed[0], summed[1][:, :, :192]], axis=2)
    result = 0.2 * math.sqrt(width) * (A1 * momentum.astype(F32) + product)
    return result.astype(BF16)


def solution(mesh):
    split = Mesh(mesh.devices.reshape(4, 2, 4, 8, 2), ("zq", "zh", "x", "y", "core"))
    placed = P(None, ZX, ("y", "core"))
    return jax.shard_map(local, mesh=split, in_specs=(placed,), out_specs=placed, check_vma=False)
```

```python
import math

import jax
import jax.numpy as jnp
from jax import lax
from jax.experimental import pallas as pl
from jax.experimental.pallas import tpu as pltpu
from jax.sharding import Mesh, PartitionSpec as P

F32 = jnp.float32
BF16 = jnp.bfloat16
A1, A3, A5 = 3.4445, -4.775, 2.0315
Z = ("zl", "zh")
XZ = ("x", "zl", "zh")
HY = ("zh", "y")
VMEM = pl.BlockSpec(memory_space=pltpu.VMEM)


def kernel_call(body, inputs, shape, dtype, flops):
    return kernel_calls(body, inputs, [jax.ShapeDtypeStruct(shape, dtype)], flops)[0]


def kernel_calls(body, inputs, outputs, flops):
    return pl.pallas_call(
        body,
        out_shape=outputs,
        in_specs=[VMEM] * len(inputs),
        out_specs=[VMEM] * len(outputs),
        cost_estimate=pl.CostEstimate(flops=flops, bytes_accessed=0, transcendentals=0),
        compiler_params=pltpu.CompilerParams(vmem_limit_bytes=40 * 2**20),
    )(*inputs)


def swap(array):
    return lax.ppermute(array, "core", [(0, 1), (1, 0)])


def exchange(array, axes):
    return lax.all_to_all(array, axes, 0, 0, tiled=True)


def first_block(other):
    core = lax.axis_index("core")
    return lax.axis_index("x") * 8 + (1 - core if other else core) * 4


def pack_body(momentum, sent, kept):
    for layer in range(4):
        sent[layer * 2] = momentum[layer, :, :224]
        sent[layer * 2 + 1] = momentum[layer, :, 224:]
    kept[...] = momentum[...]


def gram_body(other):
    def body(m, out):
        rows = m[pl.ds(first_block(other), 4)].reshape(192, 224)
        for cg in range(4):
            columns = m[cg * 8 : cg * 8 + 8].reshape(384, 224)
            block = lax.dot_general(
                rows, columns, (((1,), (1,)), ((), ())), preferred_element_type=F32
            )
            for rg in range(4):
                out[rg * 4 + cg] = block[rg * 48 : rg * 48 + 48].astype(out.dtype)

    return body


def product_terms(m, tiles, other):
    panels = [jnp.concatenate([tiles[rg * 4 + cg] for rg in range(4)], axis=0) for cg in range(4)]
    gm = jnp.zeros((192, 224), F32)
    for cg in range(4):
        rows = m[cg * 8 : cg * 8 + 8].reshape(384, 224)
        gm = gm + jnp.dot(panels[cg], rows, preferred_element_type=F32)
    own = m[pl.ds(first_block(other), 4)].reshape(192, 224).astype(F32)
    w = (A3 * own + A5 * gm).astype(BF16)
    for cg in range(4):
        yield lax.dot_general(panels[cg], w, (((0,), (0,)), ((), ())), preferred_element_type=F32)


def product_body(m, tiles, out):
    for cg, piece in enumerate(product_terms(m, tiles, False)):
        out[cg * 8 : cg * 8 + 8] = piece.reshape(8, 48, 224)


def product_add_body(m, tiles, partial, out):
    for cg, piece in enumerate(product_terms(m, tiles, True)):
        block = slice(cg * 8, cg * 8 + 8)
        out[block] = (partial[block] + piece.reshape(8, 48, 224)).astype(BF16)


def local(momentum):
    width = 7168
    packed = jax.ShapeDtypeStruct((8, 48, 224), BF16)
    kept = jax.ShapeDtypeStruct(momentum.shape, BF16)
    sent, kept = kernel_calls(pack_body, [momentum], [packed, kept], 10**6)
    m = lax.all_gather(exchange(sent, Z), "x", axis=0, tiled=True)

    gram_flops = 2 * 192 * 1536 * 224
    away = swap(kernel_call(gram_body(True), [m], (16, 48, 384), BF16, gram_flops))
    own = kernel_call(gram_body(False), [m], (16, 48, 384), F32, gram_flops)
    part = (own + away.astype(F32)).astype(BF16)
    parts = exchange(part, HY)
    tile = jnp.sum(parts.astype(F32), axis=0).astype(BF16)
    gathered = exchange(jnp.broadcast_to(tile[None], (16, 48, 384)), HY)

    others = swap(gathered)
    partial = kernel_call(product_body, [m, gathered], (32, 48, 224), F32, 2 * gram_flops)
    total = kernel_call(
        product_add_body, [m, others, partial], (32, 48, 224), BF16, 2 * gram_flops
    )
    back = exchange(total, XZ)
    summed = jnp.sum(back.reshape(4, 4, 2, 48, 224).astype(F32), axis=0)
    product = jnp.concatenate([summed[:, 0], summed[:, 1]], axis=2)
    result = 0.2 * math.sqrt(width) * (A1 * kept.astype(F32) + product)
    return result.astype(BF16)


def solution(mesh):
    split = Mesh(mesh.devices.reshape(4, 2, 4, 8, 2), ("zl", "zh", "x", "y", "core"))
    placed = P(None, ("zl", "zh", "x"), ("y", "core"))
    return jax.shard_map(local, mesh=split, in_specs=(placed,), out_specs=placed, check_vma=False)
```

```python
import math

import jax
import jax.numpy as jnp
from jax import lax
from jax.experimental import pallas as pl
from jax.experimental.pallas import tpu as pltpu
from jax.sharding import Mesh, PartitionSpec as P

F32 = jnp.float32
BF16 = jnp.bfloat16
A1, A3, A5 = 3.4445, -4.775, 2.0315
Z = ("zl", "zh")
HY = ("zh", "y")
VMEM = pl.BlockSpec(memory_space=pltpu.VMEM)


def kernel_call(body, inputs, shape, dtype, flops):
    return kernel_calls(body, inputs, [jax.ShapeDtypeStruct(shape, dtype)], flops)[0]


def kernel_calls(body, inputs, outputs, flops):
    return pl.pallas_call(
        body,
        out_shape=outputs,
        in_specs=[VMEM] * len(inputs),
        out_specs=[VMEM] * len(outputs),
        cost_estimate=pl.CostEstimate(flops=flops, bytes_accessed=0, transcendentals=0),
        compiler_params=pltpu.CompilerParams(vmem_limit_bytes=40 * 2**20),
    )(*inputs)


def swap(array):
    return lax.ppermute(array, "core", [(0, 1), (1, 0)])


def exchange(array, axes):
    return lax.all_to_all(array, axes, 0, 0, tiled=True)


def first_block(other):
    core = lax.axis_index("core")
    return lax.axis_index("x") * 8 + (1 - core if other else core) * 4


def pack_body(momentum, sent, kept):
    for layer in range(4):
        sent[layer * 2] = momentum[layer, :, :224]
        sent[layer * 2 + 1] = momentum[layer, :, 224:]
    kept[...] = momentum[...]


def gram_body(other):
    def body(m, out):
        rows = m[pl.ds(first_block(other), 4)].reshape(192, 224)
        for cg in range(4):
            columns = m[cg * 8 : cg * 8 + 8].reshape(384, 224)
            block = lax.dot_general(
                rows, columns, (((1,), (1,)), ((), ())), preferred_element_type=F32
            )
            for rg in range(4):
                out[rg * 4 + cg] = block[rg * 48 : rg * 48 + 48].astype(out.dtype)

    return body


def panel(tiles):
    return [jnp.concatenate([tiles[rg * 4 + cg] for rg in range(4)], axis=0) for cg in range(4)]


def times(tiles, m):
    total = jnp.zeros((192, 224), F32)
    for cg, piece in enumerate(panel(tiles)):
        rows = m[cg * 8 : cg * 8 + 8].reshape(384, 224)
        total = total + jnp.dot(piece, rows, preferred_element_type=F32)
    return total


def weight(m, tiles, other):
    rows = m[pl.ds(first_block(other), 4)].reshape(192, 224).astype(F32)
    return (A3 * rows + A5 * times(tiles, m)).astype(BF16).reshape(4, 48, 224)


def weight_body(m, tiles, out):
    out[...] = weight(m, tiles, False)


def weight_both_body(m, tiles, own, out):
    core = lax.axis_index("core")
    out[pl.ds(core * 4, 4)] = own[...]
    out[pl.ds((1 - core) * 4, 4)] = weight(m, tiles, True)


def product_body(w, tiles, others, out):
    core = lax.axis_index("core")
    out[pl.ds(core * 4, 4)] = times(tiles, w).astype(BF16).reshape(4, 48, 224)
    out[pl.ds((1 - core) * 4, 4)] = times(others, w).astype(BF16).reshape(4, 48, 224)


def local(momentum):
    width = 7168
    packed = jax.ShapeDtypeStruct((8, 48, 224), BF16)
    kept = jax.ShapeDtypeStruct(momentum.shape, BF16)
    sent, kept = kernel_calls(pack_body, [momentum], [packed, kept], 10**6)
    m = lax.all_gather(exchange(sent, Z), "x", axis=0, tiled=True)

    gram_flops = 2 * 192 * 1536 * 224
    away = swap(kernel_call(gram_body(True), [m], (16, 48, 384), BF16, gram_flops))
    own = kernel_call(gram_body(False), [m], (16, 48, 384), F32, gram_flops)
    part = (own + away.astype(F32)).astype(BF16)
    parts = exchange(part, HY)
    tile = jnp.sum(parts.astype(F32), axis=0).astype(BF16)
    gathered = exchange(jnp.broadcast_to(tile[None], (16, 48, 384)), HY)

    others = swap(gathered)
    own = kernel_call(weight_body, [m, gathered], (4, 48, 224), BF16, gram_flops)
    both = kernel_call(weight_both_body, [m, others, own], (8, 48, 224), BF16, gram_flops)
    w = lax.all_gather(both, "x", axis=0, tiled=True)
    rows = kernel_call(product_body, [w, gathered, others], (8, 48, 224), BF16, 2 * gram_flops)
    back = exchange(rows, Z).reshape(4, 2, 48, 224).astype(F32)
    product = jnp.concatenate([back[:, 0], back[:, 1]], axis=2)
    result = 0.2 * math.sqrt(width) * (A1 * kept.astype(F32) + product)
    return result.astype(BF16)


def solution(mesh):
    split = Mesh(mesh.devices.reshape(4, 2, 4, 8, 2), ("zl", "zh", "x", "y", "core"))
    placed = P(None, ("zl", "zh", "x"), ("y", "core"))
    return jax.shard_map(local, mesh=split, in_specs=(placed,), out_specs=placed, check_vma=False)
```

```python
import math

import jax
import jax.numpy as jnp
from jax import lax
from jax.experimental import pallas as pl
from jax.experimental.pallas import tpu as pltpu
from jax.sharding import Mesh, PartitionSpec as P

F32 = jnp.float32
BF16 = jnp.bfloat16
A1, A3, A5 = 3.4445, -4.775, 2.0315
SCALE = 0.2 * math.sqrt(7168)
Z = ("zl", "zh")
HY = ("zh", "y")
VMEM = pl.BlockSpec(memory_space=pltpu.VMEM)


def kernel_call(body, inputs, shape, dtype, flops):
    return pl.pallas_call(
        body,
        out_shape=jax.ShapeDtypeStruct(shape, dtype),
        in_specs=[VMEM] * len(inputs),
        out_specs=VMEM,
        cost_estimate=pl.CostEstimate(flops=flops, bytes_accessed=0, transcendentals=0),
        compiler_params=pltpu.CompilerParams(vmem_limit_bytes=40 * 2**20),
    )(*inputs)


def swap(array):
    return lax.ppermute(array, "core", [(0, 1), (1, 0)])


def exchange(array, axes):
    return lax.all_to_all(array, axes, 0, 0, tiled=True)


def first_block(other):
    core = lax.axis_index("core")
    return lax.axis_index("x") * 8 + (1 - core if other else core) * 4


def pack_body(momentum, sent, kept, arrived):
    copies = [
        pltpu.make_async_copy(momentum.at[layer], kept.at[layer], arrived.at[layer])
        for layer in range(4)
    ]
    for copy in copies:
        copy.start()
    for layer in range(4):
        copies[layer].wait()
        sent[layer * 2] = kept[layer, :, :224]
        sent[layer * 2 + 1] = kept[layer, :, 224:]


def pack(momentum):
    return pl.pallas_call(
        pack_body,
        out_shape=[
            jax.ShapeDtypeStruct((8, 48, 224), BF16),
            jax.ShapeDtypeStruct(momentum.shape, BF16),
        ],
        in_specs=[pl.BlockSpec(memory_space=pltpu.HBM)],
        out_specs=[VMEM, VMEM],
        scratch_shapes=[pltpu.SemaphoreType.DMA((4,))],
    )(momentum)


def finish_body(kept, back, out, held, left):
    copies = []
    for layer in range(4):
        product = jnp.concatenate([back[layer * 2], back[layer * 2 + 1]], axis=1).astype(F32)
        result = SCALE * (A1 * kept[layer].astype(F32) + product)
        held[layer] = result.astype(BF16)
        copies.append(pltpu.make_async_copy(held.at[layer], out.at[layer], left.at[layer]))
        copies[layer].start()
    for copy in copies:
        copy.wait()


def finish(kept, back):
    return pl.pallas_call(
        finish_body,
        out_shape=jax.ShapeDtypeStruct(kept.shape, BF16),
        in_specs=[VMEM, VMEM],
        out_specs=pl.BlockSpec(memory_space=pltpu.HBM),
        scratch_shapes=[pltpu.VMEM(kept.shape, BF16), pltpu.SemaphoreType.DMA((4,))],
    )(kept, back)


def gram_body(other):
    def body(m, out):
        rows = m[pl.ds(first_block(other), 4)].reshape(192, 224)
        for cg in range(4):
            columns = m[cg * 8 : cg * 8 + 8].reshape(384, 224)
            block = lax.dot_general(
                rows, columns, (((1,), (1,)), ((), ())), preferred_element_type=F32
            )
            for rg in range(4):
                out[rg * 4 + cg] = block[rg * 48 : rg * 48 + 48].astype(out.dtype)

    return body


def panel(tiles):
    return [jnp.concatenate([tiles[rg * 4 + cg] for rg in range(4)], axis=0) for cg in range(4)]


def times(tiles, m):
    total = jnp.zeros((192, 224), F32)
    for cg, piece in enumerate(panel(tiles)):
        rows = m[cg * 8 : cg * 8 + 8].reshape(384, 224)
        total = total + jnp.dot(piece, rows, preferred_element_type=F32)
    return total


def weight(m, tiles, other):
    rows = m[pl.ds(first_block(other), 4)].reshape(192, 224).astype(F32)
    return (A3 * rows + A5 * times(tiles, m)).astype(BF16).reshape(4, 48, 224)


def weight_body(m, tiles, out):
    out[...] = weight(m, tiles, False)


def weight_both_body(m, tiles, own, out):
    core = lax.axis_index("core")
    out[pl.ds(core * 4, 4)] = own[...]
    out[pl.ds((1 - core) * 4, 4)] = weight(m, tiles, True)


def product_body(w, tiles, others, out):
    core = lax.axis_index("core")
    out[pl.ds(core * 4, 4)] = times(tiles, w).astype(BF16).reshape(4, 48, 224)
    out[pl.ds((1 - core) * 4, 4)] = times(others, w).astype(BF16).reshape(4, 48, 224)


def local(momentum):
    sent, kept = pack(momentum)
    m = lax.all_gather(exchange(sent, Z), "x", axis=0, tiled=True)

    gram_flops = 2 * 192 * 1536 * 224
    away = swap(kernel_call(gram_body(True), [m], (16, 48, 384), BF16, gram_flops))
    own = kernel_call(gram_body(False), [m], (16, 48, 384), F32, gram_flops)
    part = (own + away.astype(F32)).astype(BF16)
    parts = exchange(part, HY)
    tile = jnp.sum(parts.astype(F32), axis=0).astype(BF16)
    gathered = exchange(jnp.broadcast_to(tile[None], (16, 48, 384)), HY)

    others = swap(gathered)
    own = kernel_call(weight_body, [m, gathered], (4, 48, 224), BF16, gram_flops)
    both = kernel_call(weight_both_body, [m, others, own], (8, 48, 224), BF16, gram_flops)
    w = lax.all_gather(both, "x", axis=0, tiled=True)
    rows = kernel_call(product_body, [w, gathered, others], (8, 48, 224), BF16, 2 * gram_flops)
    return finish(kept, exchange(rows, Z))


def solution(mesh):
    split = Mesh(mesh.devices.reshape(4, 2, 4, 8, 2), ("zl", "zh", "x", "y", "core"))
    placed = P(None, ("zl", "zh", "x"), ("y", "core"))
    return jax.shard_map(local, mesh=split, in_specs=(placed,), out_specs=placed, check_vma=False)
```

```python
import math

import jax
import jax.numpy as jnp
from jax import lax
from jax.experimental import pallas as pl
from jax.experimental.pallas import tpu as pltpu
from jax.sharding import Mesh, PartitionSpec as P

F32 = jnp.float32
BF16 = jnp.bfloat16
A1, A3, A5 = 3.4445, -4.775, 2.0315
Z = ("zl", "zh")
HY = ("zh", "y")
VMEM = pl.BlockSpec(memory_space=pltpu.VMEM)


def kernel_call(body, inputs, shape, dtype, flops):
    return kernel_calls(body, inputs, [jax.ShapeDtypeStruct(shape, dtype)], flops)[0]


def kernel_calls(body, inputs, outputs, flops):
    return pl.pallas_call(
        body,
        out_shape=outputs,
        in_specs=[VMEM] * len(inputs),
        out_specs=[VMEM] * len(outputs),
        cost_estimate=pl.CostEstimate(flops=flops, bytes_accessed=0, transcendentals=0),
        compiler_params=pltpu.CompilerParams(vmem_limit_bytes=40 * 2**20),
    )(*inputs)


def swap(array):
    return lax.ppermute(array, "core", [(0, 1), (1, 0)])


def exchange(array, axes):
    return lax.all_to_all(array, axes, 0, 0, tiled=True)


def half(m, x, h):
    return m[pl.ds(x * 8 + h * 4, 4)]


def half_rows(m, group, h):
    return jnp.concatenate([half(m, 2 * group + i, h) for i in range(2)]).reshape(384, 224)


def pack_body(momentum, sent, kept):
    for layer in range(4):
        sent[layer * 2] = momentum[layer, :, :224]
        sent[layer * 2 + 1] = momentum[layer, :, 224:]
    kept[...] = momentum[...]


def send_body(m, out):
    core = lax.axis_index("core")
    for x in range(4):
        out[x * 4 : x * 4 + 4] = half(m, x, 1 - core)
    out[16:20] = half(m, lax.axis_index("x"), core)


def gram_body(m, got, out):
    core, x = lax.axis_index("core"), lax.axis_index("x")
    other = 1 - core
    theirs = got.at[other]

    def product(rows, columns):
        return lax.dot_general(
            rows, columns, (((1,), (1,)), ((), ())), preferred_element_type=F32
        )

    for h, far in ((core, theirs[pl.ds(x * 4, 4)]), (other, theirs[16:20])):
        near = half(m, x, h).reshape(192, 224)
        far = far.reshape(192, 224)
        for group in range(2):
            block = product(near, half_rows(m, group, core))
            block = block + product(far, theirs[group * 8 : group * 8 + 8].reshape(384, 224))
            out[pl.ds(h * 4, 4), group] = block.astype(BF16).reshape(4, 48, 384)


def times(tiles, m, h):
    total = jnp.zeros((384, 224), F32)
    for group in range(2):
        panel = jnp.concatenate([tiles[2 * block + group] for block in range(8)], axis=0)
        total = total + jnp.dot(panel, half_rows(m, group, h), preferred_element_type=F32)
    return total.reshape(8, 48, 224)


def first_body(m, tiles, out):
    out[...] = times(tiles, m, lax.axis_index("core"))


def weight_body(m, others, first, out):
    gm = first[...] + times(others, m, 1 - lax.axis_index("core"))
    own = m[pl.ds(lax.axis_index("x") * 8, 8)].astype(F32)
    out[...] = (A3 * own + A5 * gm).astype(BF16)


def product_body(w, tiles, others, out):
    core = lax.axis_index("core")
    out[...] = (times(tiles, w, core) + times(others, w, 1 - core)).astype(BF16)


def local(momentum):
    width = 7168
    packed = jax.ShapeDtypeStruct((8, 48, 224), BF16)
    kept = jax.ShapeDtypeStruct(momentum.shape, BF16)
    sent, kept = kernel_calls(pack_body, [momentum], [packed, kept], 10**6)
    m = lax.all_gather(exchange(sent, Z), "x", axis=0, tiled=True)

    flops = 2 * 384 * 768 * 224
    send = kernel_call(send_body, [m], (20, 48, 224), BF16, 10**6)
    got = lax.all_gather(send, "core", axis=0)
    part = kernel_call(gram_body, [m, got], (8, 2, 48, 384), BF16, 2 * flops)
    parts = exchange(part.reshape(16, 48, 384), HY)
    tile = jnp.sum(parts.astype(F32), axis=0).astype(BF16)
    gathered = exchange(jnp.broadcast_to(tile[None], (16, 48, 384)), HY)

    others = swap(gathered)
    first = kernel_call(first_body, [m, gathered], (8, 48, 224), F32, flops)
    both = kernel_call(weight_body, [m, others, first], (8, 48, 224), BF16, flops)
    w = lax.all_gather(both, "x", axis=0, tiled=True)
    rows = kernel_call(product_body, [w, gathered, others], (8, 48, 224), BF16, 2 * flops)
    back = exchange(rows, Z).reshape(4, 2, 48, 224).astype(F32)
    product = jnp.concatenate([back[:, 0], back[:, 1]], axis=2)
    result = 0.2 * math.sqrt(width) * (A1 * kept.astype(F32) + product)
    return result.astype(BF16)


def solution(mesh):
    split = Mesh(mesh.devices.reshape(4, 2, 4, 8, 2), ("zl", "zh", "x", "y", "core"))
    placed = P(None, ("zl", "zh", "x"), ("y", "core"))
    return jax.shard_map(local, mesh=split, in_specs=(placed,), out_specs=placed, check_vma=False)
```

```python
import math

import jax
import jax.numpy as jnp
from jax import lax
from jax.experimental import pallas as pl
from jax.experimental.pallas import tpu as pltpu
from jax.sharding import Mesh, PartitionSpec as P

F32 = jnp.float32
BF16 = jnp.bfloat16
A1, A3, A5 = 3.4445, -4.775, 2.0315
Z = ("zl", "zh")
HY = ("zh", "y")
VMEM = pl.BlockSpec(memory_space=pltpu.VMEM)


def kernel_call(body, inputs, shape, dtype, flops, scratch=()):
    return kernel_calls(body, inputs, [shape], dtype, flops, scratch)[0]


def kernel_calls(body, inputs, shapes, dtype, flops, scratch=()):
    return pl.pallas_call(
        body,
        out_shape=[jax.ShapeDtypeStruct(shape, dtype) for shape in shapes],
        in_specs=[VMEM] * len(inputs),
        out_specs=[VMEM] * len(shapes),
        scratch_shapes=scratch,
        cost_estimate=pl.CostEstimate(flops=flops, bytes_accessed=0, transcendentals=0),
        compiler_params=pltpu.CompilerParams(vmem_limit_bytes=40 * 2**20),
    )(*inputs)


def swap(array):
    return lax.ppermute(array, "core", [(0, 1), (1, 0)])


def exchange(array, axes):
    return lax.all_to_all(array, axes, 0, 0, tiled=True)


def half(m, x, h):
    return m[pl.ds(x * 8 + h * 4, 4)]


def half_rows(m, group, h):
    return jnp.concatenate([half(m, 2 * group + i, h) for i in range(2)]).reshape(384, 224)


def pack_body(momentum, sent, kept):
    for layer in range(4):
        sent[layer * 2] = momentum[layer, :, :224]
        sent[layer * 2 + 1] = momentum[layer, :, 224:]
    kept[...] = momentum[...]


def squeeze(blocks, out):
    for z in range(8):
        out[z] = blocks[z][:, :128]
    for h in range(2):
        tails = jnp.concatenate([blocks[h * 4 + i][:, 128:] for i in range(4)], axis=1)
        for k in range(3):
            out[8 + h * 3 + k] = tails[:, k * 128 : k * 128 + 128]


def unsqueeze(packed, m):
    for x in range(4):
        for h in range(2):
            tails = jnp.concatenate([packed[x * 14 + 8 + h * 3 + k] for k in range(3)], axis=1)
            for i in range(4):
                head = packed[x * 14 + h * 4 + i]
                tail = tails[:, i * 96 : i * 96 + 96]
                m[x * 8 + h * 4 + i] = jnp.concatenate([head, tail], axis=1)


def squeeze_body(blocks, out):
    squeeze([blocks[z] for z in range(8)], out)


def spread_body(packed, m, out):
    unsqueeze(packed, m)
    core = lax.axis_index("core")
    for x in range(4):
        out[x * 4 : x * 4 + 4] = half(m, x, 1 - core)
    out[16:20] = half(m, lax.axis_index("x"), core)


def gram_body(m, got, out):
    core, x = lax.axis_index("core"), lax.axis_index("x")
    other = 1 - core
    theirs = got.at[other]

    def product(rows, columns):
        return lax.dot_general(
            rows, columns, (((1,), (1,)), ((), ())), preferred_element_type=F32
        )

    for h, far in ((core, theirs[pl.ds(x * 4, 4)]), (other, theirs[16:20])):
        near = half(m, x, h).reshape(192, 224)
        far = far.reshape(192, 224)
        for group in range(2):
            block = product(near, half_rows(m, group, core))
            block = block + product(far, theirs[group * 8 : group * 8 + 8].reshape(384, 224))
            out[pl.ds(h * 4, 4), group] = block.astype(BF16).reshape(4, 48, 384)


def times(tiles, m, h):
    total = jnp.zeros((384, 224), F32)
    for group in range(2):
        panel = jnp.concatenate([tiles[2 * block + group] for block in range(8)], axis=0)
        total = total + jnp.dot(panel, half_rows(m, group, h), preferred_element_type=F32)
    return total.reshape(8, 48, 224)


def first_body(m, tiles, out):
    out[...] = times(tiles, m, lax.axis_index("core"))


def weight_body(m, others, first, out):
    gm = first[...] + times(others, m, 1 - lax.axis_index("core"))
    own = m[pl.ds(lax.axis_index("x") * 8, 8)].astype(F32)
    w = (A3 * own + A5 * gm).astype(BF16)
    squeeze([w[z] for z in range(8)], out)


def product_body(packed, tiles, others, out, w):
    unsqueeze(packed, w)
    core = lax.axis_index("core")
    out[...] = (times(tiles, w, core) + times(others, w, 1 - core)).astype(BF16)


def local(momentum):
    width = 7168
    sent, kept = kernel_calls(
        pack_body, [momentum], [(8, 48, 224), momentum.shape], BF16, 10**6
    )
    packed = kernel_call(squeeze_body, [exchange(sent, Z)], (14, 48, 128), BF16, 10**6)
    m, send = kernel_calls(
        spread_body,
        [lax.all_gather(packed, "x", axis=0, tiled=True)],
        [(32, 48, 224), (20, 48, 224)],
        BF16,
        10**6,
    )

    flops = 2 * 384 * 768 * 224
    got = lax.all_gather(send, "core", axis=0)
    part = kernel_call(gram_body, [m, got], (8, 2, 48, 384), BF16, 2 * flops)
    parts = exchange(part.reshape(16, 48, 384), HY)
    tile = jnp.sum(parts.astype(F32), axis=0).astype(BF16)
    gathered = exchange(jnp.broadcast_to(tile[None], (16, 48, 384)), HY)

    others = swap(gathered)
    first = kernel_call(first_body, [m, gathered], (8, 48, 224), F32, flops)
    both = kernel_call(weight_body, [m, others, first], (14, 48, 128), BF16, flops)
    w = lax.all_gather(both, "x", axis=0, tiled=True)
    whole = [pltpu.VMEM((32, 48, 224), BF16)]
    rows = kernel_call(
        product_body, [w, gathered, others], (8, 48, 224), BF16, 2 * flops, scratch=whole
    )
    back = exchange(rows, Z).reshape(4, 2, 48, 224).astype(F32)
    product = jnp.concatenate([back[:, 0], back[:, 1]], axis=2)
    result = 0.2 * math.sqrt(width) * (A1 * kept.astype(F32) + product)
    return result.astype(BF16)


def solution(mesh):
    split = Mesh(mesh.devices.reshape(4, 2, 4, 8, 2), ("zl", "zh", "x", "y", "core"))
    placed = P(None, ("zl", "zh", "x"), ("y", "core"))
    return jax.shard_map(local, mesh=split, in_specs=(placed,), out_specs=placed, check_vma=False)
```

```python
import math

import jax
import jax.numpy as jnp
from jax import lax
from jax.experimental import pallas as pl
from jax.experimental.pallas import tpu as pltpu
from jax.sharding import Mesh, PartitionSpec as P

F32 = jnp.float32
BF16 = jnp.bfloat16
A1, A3, A5 = 3.4445, -4.775, 2.0315
Z = ("zl", "zh")
HY = ("zh", "y")
VMEM = pl.BlockSpec(memory_space=pltpu.VMEM)


def kernel_call(body, inputs, shape, dtype, flops):
    return kernel_calls(body, inputs, [jax.ShapeDtypeStruct(shape, dtype)], flops)[0]


def kernel_calls(body, inputs, outputs, flops):
    return pl.pallas_call(
        body,
        out_shape=outputs,
        in_specs=[VMEM] * len(inputs),
        out_specs=[VMEM] * len(outputs),
        cost_estimate=pl.CostEstimate(flops=flops, bytes_accessed=0, transcendentals=0),
        compiler_params=pltpu.CompilerParams(vmem_limit_bytes=40 * 2**20),
    )(*inputs)


def swap(array):
    return lax.ppermute(array, "core", [(0, 1), (1, 0)])


def exchange(array, axes):
    return lax.all_to_all(array, axes, 0, 0, tiled=True)


def stack(blocks):
    return jnp.concatenate([block.reshape(192, 224) for block in blocks], axis=0)


def pack_body(momentum, sent, kept):
    for layer in range(4):
        sent[layer * 2] = momentum[layer, :, :224]
        sent[layer * 2 + 1] = momentum[layer, :, 224:]
    kept[...] = momentum[...]


def shard_body(both, out):
    for columns in range(2):
        out[columns] = both[columns, pl.ds(lax.axis_index("core") * 4, 4)]


def gram_body(both, m, out):
    for group in range(2):
        total = jnp.zeros((384, 384), F32)
        for columns in range(2):
            total = total + lax.dot_general(
                both[columns].reshape(384, 224),
                stack([m[2 * group + i, columns] for i in range(2)]),
                (((1,), (1,)), ((), ())),
                preferred_element_type=F32,
            )
        out[:, group] = total.astype(BF16).reshape(8, 48, 384)


def send_body(m, out):
    out[...] = m[:, 1 - lax.axis_index("core")]


def times(tiles, groups):
    total = jnp.zeros((384, 224), F32)
    for group in range(2):
        panel = jnp.concatenate([tiles[2 * block + group] for block in range(8)], axis=0)
        total = total + jnp.dot(panel, groups[group], preferred_element_type=F32)
    return total.reshape(8, 48, 224)


def first_body(m, tiles, out):
    core = lax.axis_index("core")
    out[...] = times(tiles, [stack([m[2 * g + i, core] for i in range(2)]) for g in range(2)])


def weight_body(both, got, others, first, out):
    core = lax.axis_index("core")
    theirs = got.at[1 - core]
    groups = [stack([theirs[2 * g + i] for i in range(2)]) for g in range(2)]
    gm = first[...] + times(others, groups)
    out[...] = (A3 * both[core].astype(F32) + A5 * gm).astype(BF16)


def product_body(w, tiles, others, out):
    core = lax.axis_index("core")
    total = jnp.zeros((8, 48, 224), F32)
    for held, h in ((tiles, core), (others, 1 - core)):
        groups = [
            stack([w[2 * g + i, pl.ds(h * 4, 4)] for i in range(2)]) for g in range(2)
        ]
        total = total + times(held, groups)
    out[...] = total.astype(BF16)


def local(momentum):
    width = 7168
    packed = jax.ShapeDtypeStruct((8, 48, 224), BF16)
    kept = jax.ShapeDtypeStruct(momentum.shape, BF16)
    sent, kept = kernel_calls(pack_body, [momentum], [packed, kept], 10**6)
    flops = 2 * 384 * 768 * 224
    both = lax.all_gather(exchange(sent, Z), "core", axis=0)
    shard = kernel_call(shard_body, [both], (2, 4, 48, 224), BF16, 10**6)
    m = lax.all_gather(shard, "x", axis=0)
    part = kernel_call(gram_body, [both, m], (8, 2, 48, 384), BF16, 2 * flops)
    parts = exchange(part.reshape(16, 48, 384), HY)
    tile = jnp.sum(parts.astype(F32), axis=0).astype(BF16)
    tile, later = lax.optimization_barrier((tile, m))
    gathered = exchange(jnp.broadcast_to(tile[None], (16, 48, 384)), HY)
    send = kernel_call(send_body, [later], (4, 4, 48, 224), BF16, 10**6)
    got = lax.all_gather(send, "core", axis=0)
    gathered, got = lax.optimization_barrier((gathered, got))

    others = swap(gathered)
    first = kernel_call(first_body, [m, gathered], (8, 48, 224), F32, flops)
    weighted = kernel_call(
        weight_body, [both, got, others, first], (8, 48, 224), BF16, flops
    )
    w = lax.all_gather(weighted, "x", axis=0)
    rows = kernel_call(product_body, [w, gathered, others], (8, 48, 224), BF16, 2 * flops)
    back = exchange(rows, Z).reshape(4, 2, 48, 224).astype(F32)
    product = jnp.concatenate([back[:, 0], back[:, 1]], axis=2)
    result = 0.2 * math.sqrt(width) * (A1 * kept.astype(F32) + product)
    return result.astype(BF16)


def solution(mesh):
    split = Mesh(mesh.devices.reshape(4, 2, 4, 8, 2), ("zl", "zh", "x", "y", "core"))
    placed = P(None, ("zl", "zh", "x"), ("y", "core"))
    return jax.shard_map(local, mesh=split, in_specs=(placed,), out_specs=placed, check_vma=False)
```

```python
import math

import jax
import jax.numpy as jnp
from jax import lax
from jax.experimental import pallas as pl
from jax.experimental.pallas import tpu as pltpu
from jax.sharding import Mesh, PartitionSpec as P

F32 = jnp.float32
BF16 = jnp.bfloat16
A1, A3, A5 = 3.4445, -4.775, 2.0315
Z = ("zl", "zh")
HY = ("zh", "y")
VMEM = pl.BlockSpec(memory_space=pltpu.VMEM)


def kernel_call(body, inputs, shape, dtype, flops):
    return kernel_calls(body, inputs, [jax.ShapeDtypeStruct(shape, dtype)], flops)[0]


def kernel_calls(body, inputs, outputs, flops):
    return pl.pallas_call(
        body,
        out_shape=outputs,
        in_specs=[VMEM] * len(inputs),
        out_specs=[VMEM] * len(outputs),
        cost_estimate=pl.CostEstimate(flops=flops, bytes_accessed=0, transcendentals=0),
        compiler_params=pltpu.CompilerParams(vmem_limit_bytes=40 * 2**20),
    )(*inputs)


def swap(array):
    return lax.ppermute(array, "core", [(0, 1), (1, 0)])


def exchange(array, axes):
    return lax.all_to_all(array, axes, 0, 0, tiled=True)


def stack(blocks):
    return jnp.concatenate([block.reshape(192, 224) for block in blocks], axis=0)


def pack_body(momentum, sent, kept):
    for layer in range(4):
        sent[layer * 2] = momentum[layer, :, :224]
        sent[layer * 2 + 1] = momentum[layer, :, 224:]
    kept[...] = momentum[...]


def shard_body(both, out):
    for columns in range(2):
        out[columns] = both[columns, pl.ds(lax.axis_index("core") * 4, 4)]


def gram_body(both, m, out):
    for group in range(2):
        total = jnp.zeros((384, 384), F32)
        for columns in range(2):
            total = total + lax.dot_general(
                both[columns].reshape(384, 224),
                stack([m[2 * group + i, columns] for i in range(2)]),
                (((1,), (1,)), ((), ())),
                preferred_element_type=F32,
            )
        out[:, group] = total.astype(BF16).reshape(8, 48, 384)


def tile_body(parts, out):
    total = parts[0].astype(F32)
    for k in range(1, 16):
        total = total + parts[k].astype(F32)
    tile = total.astype(BF16)
    for k in range(16):
        out[k] = tile


def times(tiles, groups):
    total = jnp.zeros((384, 224), F32)
    for group in range(2):
        panel = jnp.concatenate([tiles[2 * block + group] for block in range(8)], axis=0)
        total = total + jnp.dot(panel, groups[group], preferred_element_type=F32)
    return total.reshape(8, 48, 224)


def gm_body(m, tiles, keep, send):
    core = lax.axis_index("core")
    for columns, out in ((1 - core, send), (core, keep)):
        groups = [stack([m[2 * g + i, columns] for i in range(2)]) for g in range(2)]
        out[...] = times(tiles, groups).astype(out.dtype)


def weight_body(both, keep, got, out):
    core = lax.axis_index("core")
    gm = keep[...] + got[1 - core].astype(F32)
    out[...] = (A3 * both[core].astype(F32) + A5 * gm).astype(BF16)


def product_body(w, tiles, others, out):
    core = lax.axis_index("core")
    total = jnp.zeros((8, 48, 224), F32)
    for held, h in ((tiles, core), (others, 1 - core)):
        groups = [
            stack([w[2 * g + i, pl.ds(h * 4, 4)] for i in range(2)]) for g in range(2)
        ]
        total = total + times(held, groups)
    out[...] = total.astype(BF16)


def local(momentum):
    width = 7168
    packed = jax.ShapeDtypeStruct((8, 48, 224), BF16)
    kept = jax.ShapeDtypeStruct(momentum.shape, BF16)
    sent, kept = kernel_calls(pack_body, [momentum], [packed, kept], 10**6)
    flops = 2 * 384 * 768 * 224
    both = lax.all_gather(exchange(sent, Z), "core", axis=0)
    shard = kernel_call(shard_body, [both], (2, 4, 48, 224), BF16, 10**6)
    m = lax.all_gather(shard, "x", axis=0)
    part = kernel_call(gram_body, [both, m], (8, 2, 48, 384), BF16, 2 * flops)
    parts = exchange(part.reshape(16, 48, 384), HY)
    copies = kernel_call(tile_body, [parts], (16, 48, 384), BF16, 10**6)
    gathered = exchange(copies, HY)

    others = swap(gathered)
    block = (8, 48, 224)
    outputs = [jax.ShapeDtypeStruct(block, F32), jax.ShapeDtypeStruct(block, BF16)]
    keep, send = kernel_calls(gm_body, [m, gathered], outputs, 2 * flops)
    got = lax.all_gather(send, "core", axis=0)
    weighted = kernel_call(weight_body, [both, keep, got], block, BF16, 10**6)
    w = lax.all_gather(weighted, "x", axis=0)
    rows = kernel_call(product_body, [w, gathered, others], (8, 48, 224), BF16, 2 * flops)
    back = exchange(rows, Z).reshape(4, 2, 48, 224).astype(F32)
    product = jnp.concatenate([back[:, 0], back[:, 1]], axis=2)
    result = 0.2 * math.sqrt(width) * (A1 * kept.astype(F32) + product)
    return result.astype(BF16)


def solution(mesh):
    split = Mesh(mesh.devices.reshape(4, 2, 4, 8, 2), ("zl", "zh", "x", "y", "core"))
    placed = P(None, ("zl", "zh", "x"), ("y", "core"))
    return jax.shard_map(local, mesh=split, in_specs=(placed,), out_specs=placed, check_vma=False)
```

```python
import math

import jax
import jax.numpy as jnp
from jax import lax
from jax.experimental import pallas as pl
from jax.experimental.pallas import tpu as pltpu
from jax.sharding import Mesh, PartitionSpec as P

F32 = jnp.float32
BF16 = jnp.bfloat16
A1, A3, A5 = 3.4445, -4.775, 2.0315
SCALE = 0.2 * math.sqrt(7168)
Z = ("zl", "zh")
HY = ("zh", "y")
VMEM = pl.BlockSpec(memory_space=pltpu.VMEM)


def kernel_call(body, inputs, shape, dtype, flops):
    return kernel_calls(body, inputs, [jax.ShapeDtypeStruct(shape, dtype)], flops)[0]


def kernel_calls(body, inputs, outputs, flops):
    return pl.pallas_call(
        body,
        out_shape=outputs,
        in_specs=[VMEM] * len(inputs),
        out_specs=[VMEM] * len(outputs),
        cost_estimate=pl.CostEstimate(flops=flops, bytes_accessed=0, transcendentals=0),
        compiler_params=pltpu.CompilerParams(vmem_limit_bytes=40 * 2**20),
    )(*inputs)


def swap(array):
    return lax.ppermute(array, "core", [(0, 1), (1, 0)])


def exchange(array, axes):
    return lax.all_to_all(array, axes, 0, 0, tiled=True)


def stack(blocks):
    return jnp.concatenate([block.reshape(192, 224) for block in blocks], axis=0)


def pack_body(momentum, sent, kept):
    for layer in range(4):
        sent[layer * 2] = momentum[layer, :, :224]
        sent[layer * 2 + 1] = momentum[layer, :, 224:]
    kept[...] = momentum[...]


def shard_body(both, out):
    for columns in range(2):
        out[columns] = both[columns, pl.ds(lax.axis_index("core") * 4, 4)]


def gram_body(both, m, out):
    for group in range(2):
        total = jnp.zeros((384, 384), F32)
        for columns in range(2):
            total = total + lax.dot_general(
                both[columns].reshape(384, 224),
                stack([m[2 * group + i, columns] for i in range(2)]),
                (((1,), (1,)), ((), ())),
                preferred_element_type=F32,
            )
        out[:, group] = total.astype(BF16).reshape(8, 48, 384)


def base_body(both, out):
    out[...] = A3 * both[lax.axis_index("core")].astype(F32)


def kept_body(kept, out):
    out[...] = SCALE * A1 * kept[...].astype(F32)


def send_body(m, out):
    out[...] = m[:, 1 - lax.axis_index("core")]


def times(tiles, groups):
    total = jnp.zeros((384, 224), F32)
    for group in range(2):
        panel = jnp.concatenate([tiles[2 * block + group] for block in range(8)], axis=0)
        total = total + jnp.dot(panel, groups[group], preferred_element_type=F32)
    return total.reshape(8, 48, 224)


def first_body(m, tiles, out):
    core = lax.axis_index("core")
    out[...] = times(tiles, [stack([m[2 * g + i, core] for i in range(2)]) for g in range(2)])


def weight_body(base, got, others, first, out):
    core = lax.axis_index("core")
    theirs = got.at[1 - core]
    groups = [stack([theirs[2 * g + i] for i in range(2)]) for g in range(2)]
    gm = first[...] + times(others, groups)
    out[...] = (base[...] + A5 * gm).astype(BF16)


def product_body(w, tiles, others, out):
    core = lax.axis_index("core")
    total = jnp.zeros((8, 48, 224), F32)
    for held, h in ((tiles, core), (others, 1 - core)):
        groups = [
            stack([w[2 * g + i, pl.ds(h * 4, 4)] for i in range(2)]) for g in range(2)
        ]
        total = total + times(held, groups)
    out[...] = total.astype(BF16)


def local(momentum):
    packed = jax.ShapeDtypeStruct((8, 48, 224), BF16)
    kept = jax.ShapeDtypeStruct(momentum.shape, BF16)
    sent, kept = kernel_calls(pack_body, [momentum], [packed, kept], 10**6)
    flops = 2 * 384 * 768 * 224
    both = lax.all_gather(exchange(sent, Z), "core", axis=0)
    shard = kernel_call(shard_body, [both], (2, 4, 48, 224), BF16, 10**6)
    m = lax.all_gather(shard, "x", axis=0)
    part = kernel_call(gram_body, [both, m], (8, 2, 48, 384), BF16, 2 * flops)
    part, early = lax.optimization_barrier((part, both))
    base = kernel_call(base_body, [early], (8, 48, 224), F32, 10**6)
    parts = exchange(part.reshape(16, 48, 384), HY)
    parts, base = lax.optimization_barrier((parts, base))
    tile = jnp.sum(parts.astype(F32), axis=0).astype(BF16)
    tile, later = lax.optimization_barrier((tile, m))
    gathered = exchange(jnp.broadcast_to(tile[None], (16, 48, 384)), HY)
    send = kernel_call(send_body, [later], (4, 4, 48, 224), BF16, 10**6)
    got = lax.all_gather(send, "core", axis=0)
    gathered, got = lax.optimization_barrier((gathered, got))

    others = swap(gathered)
    first = kernel_call(first_body, [m, gathered], (8, 48, 224), F32, flops)
    weighted = kernel_call(
        weight_body, [base, got, others, first], (8, 48, 224), BF16, flops
    )
    w = lax.all_gather(weighted, "x", axis=0)
    rows = kernel_call(product_body, [w, gathered, others], (8, 48, 224), BF16, 2 * flops)
    rows, kept = lax.optimization_barrier((rows, kept))
    scaled = kernel_call(kept_body, [kept], momentum.shape, F32, 10**6)
    back = exchange(rows, Z)
    back, scaled = lax.optimization_barrier((back, scaled))
    back = back.reshape(4, 2, 48, 224).astype(F32)
    product = jnp.concatenate([back[:, 0], back[:, 1]], axis=2)
    return (scaled + SCALE * product).astype(BF16)


def solution(mesh):
    split = Mesh(mesh.devices.reshape(4, 2, 4, 8, 2), ("zl", "zh", "x", "y", "core"))
    placed = P(None, ("zl", "zh", "x"), ("y", "core"))
    return jax.shard_map(local, mesh=split, in_specs=(placed,), out_specs=placed, check_vma=False)
```

```python
import math

import jax
import jax.numpy as jnp
from jax import lax
from jax.experimental import pallas as pl
from jax.experimental.pallas import tpu as pltpu
from jax.sharding import Mesh, PartitionSpec as P

F32 = jnp.float32
BF16 = jnp.bfloat16
A1, A3, A5 = 3.4445, -4.775, 2.0315
Z = ("zh", "zl")
HY = ("zh", "y")
VMEM = pl.BlockSpec(memory_space=pltpu.VMEM)


def kernel_call(body, inputs, shape, dtype, flops):
    return kernel_calls(body, inputs, [jax.ShapeDtypeStruct(shape, dtype)], flops)[0]


def kernel_calls(body, inputs, outputs, flops):
    return pl.pallas_call(
        body,
        out_shape=outputs,
        in_specs=[VMEM] * len(inputs),
        out_specs=[VMEM] * len(outputs),
        cost_estimate=pl.CostEstimate(flops=flops, bytes_accessed=0, transcendentals=0),
        compiler_params=pltpu.CompilerParams(vmem_limit_bytes=40 * 2**20),
    )(*inputs)


def swap(array):
    return lax.ppermute(array, "core", [(0, 1), (1, 0)])


def exchange(array, axes):
    return lax.all_to_all(array, axes, 0, 0, tiled=True)


def stack(blocks):
    return jnp.concatenate([block.reshape(192, 224) for block in blocks], axis=0)


def pack_body(momentum, sent, kept):
    for layer in range(4):
        sent[layer] = momentum[layer, :, :224]
        sent[4 + layer] = momentum[layer, :, 224:]
    kept[...] = momentum[...]


def shard_body(both, out):
    for columns in range(2):
        out[columns] = both[columns, pl.ds(lax.axis_index("core") * 4, 4)]


def gram_body(both, m, out):
    for group in range(2):
        total = jnp.zeros((384, 384), F32)
        for columns in range(2):
            total = total + lax.dot_general(
                both[columns].reshape(384, 224),
                stack([m[2 * group + i, columns] for i in range(2)]),
                (((1,), (1,)), ((), ())),
                preferred_element_type=F32,
            )
        out[:, group] = total.astype(BF16).reshape(8, 48, 384)


def send_body(m, out):
    out[...] = m[:, 1 - lax.axis_index("core")]


def times(tiles, groups):
    total = jnp.zeros((384, 224), F32)
    for group in range(2):
        panel = jnp.concatenate([tiles[2 * block + group] for block in range(8)], axis=0)
        total = total + jnp.dot(panel, groups[group], preferred_element_type=F32)
    return total.reshape(8, 48, 224)


def first_body(m, tiles, out):
    core = lax.axis_index("core")
    out[...] = times(tiles, [stack([m[2 * g + i, core] for i in range(2)]) for g in range(2)])


def weight_body(both, got, others, first, out):
    core = lax.axis_index("core")
    theirs = got.at[1 - core]
    groups = [stack([theirs[2 * g + i] for i in range(2)]) for g in range(2)]
    gm = first[...] + times(others, groups)
    out[...] = (A3 * both[core].astype(F32) + A5 * gm).astype(BF16)


def product_body(w, tiles, others, out):
    core = lax.axis_index("core")
    total = jnp.zeros((8, 48, 224), F32)
    for held, h in ((tiles, core), (others, 1 - core)):
        groups = [
            stack([w[2 * g + i, pl.ds(h * 4, 4)] for i in range(2)]) for g in range(2)
        ]
        total = total + times(held, groups)
    out[...] = total.astype(BF16)


def local(momentum):
    width = 7168
    packed = jax.ShapeDtypeStruct((8, 48, 224), BF16)
    kept = jax.ShapeDtypeStruct(momentum.shape, BF16)
    sent, kept = kernel_calls(pack_body, [momentum], [packed, kept], 10**6)
    flops = 2 * 384 * 768 * 224
    both = lax.all_gather(exchange(sent, Z), "core", axis=0)
    shard = kernel_call(shard_body, [both], (2, 4, 48, 224), BF16, 10**6)
    m = lax.all_gather(shard, "x", axis=0)
    part = kernel_call(gram_body, [both, m], (8, 2, 48, 384), BF16, 2 * flops)
    parts = exchange(part.reshape(16, 48, 384), HY)
    tile = jnp.sum(parts.astype(F32), axis=0).astype(BF16)
    tile, later = lax.optimization_barrier((tile, m))
    gathered = exchange(jnp.broadcast_to(tile[None], (16, 48, 384)), HY)
    send = kernel_call(send_body, [later], (4, 4, 48, 224), BF16, 10**6)
    got = lax.all_gather(send, "core", axis=0)
    gathered, got = lax.optimization_barrier((gathered, got))

    others = swap(gathered)
    first = kernel_call(first_body, [m, gathered], (8, 48, 224), F32, flops)
    weighted = kernel_call(
        weight_body, [both, got, others, first], (8, 48, 224), BF16, flops
    )
    w = lax.all_gather(weighted, "x", axis=0)
    rows = kernel_call(product_body, [w, gathered, others], (8, 48, 224), BF16, 2 * flops)
    back = exchange(rows, Z).reshape(2, 4, 48, 224).astype(F32)
    product = jnp.concatenate([back[0], back[1]], axis=2)
    result = 0.2 * math.sqrt(width) * (A1 * kept.astype(F32) + product)
    return result.astype(BF16)


def solution(mesh):
    split = Mesh(mesh.devices.reshape(4, 2, 4, 8, 2), ("zl", "zh", "x", "y", "core"))
    placed = P(None, ("zl", "zh", "x"), ("y", "core"))
    return jax.shard_map(local, mesh=split, in_specs=(placed,), out_specs=placed, check_vma=False)
```

```python
import math

import jax
import jax.numpy as jnp
from jax import lax
from jax.experimental import pallas as pl
from jax.experimental.pallas import tpu as pltpu
from jax.sharding import Mesh, PartitionSpec as P

F32 = jnp.float32
BF16 = jnp.bfloat16
A1, A3, A5 = 3.4445, -4.775, 2.0315
Z = ("z0", "z1", "z2")
HY = ("y1", "y0", "y2", "z0")
X = ("x1", "x0")
AXES = ("z2", "z1", "z0", "x1", "x0", "y2", "y1", "y0", "core")
VMEM = pl.BlockSpec(memory_space=pltpu.VMEM)


def kernel_call(body, inputs, shape, dtype, flops):
    return kernel_calls(body, inputs, [jax.ShapeDtypeStruct(shape, dtype)], flops)[0]


def kernel_calls(body, inputs, outputs, flops):
    return pl.pallas_call(
        body,
        out_shape=outputs,
        in_specs=[VMEM] * len(inputs),
        out_specs=[VMEM] * len(outputs),
        cost_estimate=pl.CostEstimate(flops=flops, bytes_accessed=0, transcendentals=0),
        compiler_params=pltpu.CompilerParams(vmem_limit_bytes=40 * 2**20),
    )(*inputs)


def swap(array):
    return lax.ppermute(array, "core", [(0, 1), (1, 0)])


def exchange(array, axes):
    return lax.all_to_all(array, axes, 0, 0, tiled=True)


def stack(blocks):
    return jnp.concatenate([block.reshape(192, 224) for block in blocks], axis=0)


def places():
    for member in range(8):
        bit = {name: member >> (2 - at) & 1 for at, name in enumerate(Z)}
        yield member, bit["z2"] * 2 + bit["z1"], bit["z0"]


def pack_body(momentum, sent, kept):
    for member, layer, h in places():
        sent[member] = momentum[layer, :, h * 224 : h * 224 + 224]
    kept[...] = momentum[...]


def shard_body(both, out):
    for columns in range(2):
        out[columns] = both[columns, pl.ds(lax.axis_index("core") * 4, 4)]


def gram_body(both, m, out):
    for group in range(2):
        total = jnp.zeros((384, 384), F32)
        for columns in range(2):
            total = total + lax.dot_general(
                both[columns].reshape(384, 224),
                stack([m[2 * group + i, columns] for i in range(2)]),
                (((1,), (1,)), ((), ())),
                preferred_element_type=F32,
            )
        out[:, group] = total.astype(BF16).reshape(8, 48, 384)


def send_body(m, out):
    out[...] = m[:, 1 - lax.axis_index("core")]


def times(tiles, groups):
    total = jnp.zeros((384, 224), F32)
    for group in range(2):
        panel = jnp.concatenate([tiles[2 * block + group] for block in range(8)], axis=0)
        total = total + jnp.dot(panel, groups[group], preferred_element_type=F32)
    return total.reshape(8, 48, 224)


def first_body(m, tiles, out):
    core = lax.axis_index("core")
    out[...] = times(tiles, [stack([m[2 * g + i, core] for i in range(2)]) for g in range(2)])


def weight_body(both, got, others, first, out):
    core = lax.axis_index("core")
    theirs = got.at[1 - core]
    groups = [stack([theirs[2 * g + i] for i in range(2)]) for g in range(2)]
    gm = first[...] + times(others, groups)
    out[...] = (A3 * both[core].astype(F32) + A5 * gm).astype(BF16)


def product_body(w, tiles, others, out):
    core = lax.axis_index("core")
    total = jnp.zeros((8, 48, 224), F32)
    for held, h in ((tiles, core), (others, 1 - core)):
        groups = [
            stack([w[2 * g + i, pl.ds(h * 4, 4)] for i in range(2)]) for g in range(2)
        ]
        total = total + times(held, groups)
    out[...] = total.astype(BF16)


def local(momentum):
    width = 7168
    packed = jax.ShapeDtypeStruct((8, 48, 224), BF16)
    kept = jax.ShapeDtypeStruct(momentum.shape, BF16)
    sent, kept = kernel_calls(pack_body, [momentum], [packed, kept], 10**6)
    flops = 2 * 384 * 768 * 224
    both = lax.all_gather(exchange(sent, Z), "core", axis=0)
    shard = kernel_call(shard_body, [both], (2, 4, 48, 224), BF16, 10**6)
    m = lax.all_gather(shard, X, axis=0)
    part = kernel_call(gram_body, [both, m], (8, 2, 48, 384), BF16, 2 * flops)
    parts = exchange(part.reshape(16, 48, 384), HY)
    tile = jnp.sum(parts.astype(F32), axis=0).astype(BF16)
    tile, later = lax.optimization_barrier((tile, m))
    gathered = exchange(jnp.broadcast_to(tile[None], (16, 48, 384)), HY)
    send = kernel_call(send_body, [later], (4, 4, 48, 224), BF16, 10**6)
    got = lax.all_gather(send, "core", axis=0)
    gathered, got = lax.optimization_barrier((gathered, got))

    others = swap(gathered)
    first = kernel_call(first_body, [m, gathered], (8, 48, 224), F32, flops)
    weighted = kernel_call(
        weight_body, [both, got, others, first], (8, 48, 224), BF16, flops
    )
    w = lax.all_gather(weighted, X, axis=0)
    rows = kernel_call(product_body, [w, gathered, others], (8, 48, 224), BF16, 2 * flops)
    back = exchange(rows, Z).astype(F32)
    at = {(layer, h): member for member, layer, h in places()}
    halves = [[back[at[layer, h]] for layer in range(4)] for h in range(2)]
    product = jnp.concatenate([jnp.stack(half) for half in halves], axis=2)
    result = 0.2 * math.sqrt(width) * (A1 * kept.astype(F32) + product)
    return result.astype(BF16)


def solution(mesh):
    split = Mesh(mesh.devices.reshape((2,) * 9), AXES)
    placed = P(None, AXES[:5], AXES[5:])
    return jax.shard_map(local, mesh=split, in_specs=(placed,), out_specs=placed, check_vma=False)
```

```python
import math

import jax
import jax.numpy as jnp
from jax import lax
from jax.experimental import pallas as pl
from jax.experimental.pallas import tpu as pltpu
from jax.sharding import Mesh, PartitionSpec as P

F32 = jnp.float32
BF16 = jnp.bfloat16
A1, A3, A5 = 3.4445, -4.775, 2.0315
Z = ("z0", "z1", "z2")
HY = ("z0", "y2", "y1", "y0")
X = ("x1", "x0")
AXES = ("z2", "z1", "z0", "x1", "x0", "y2", "y1", "y0", "core")
VMEM = pl.BlockSpec(memory_space=pltpu.VMEM)


def kernel_call(body, inputs, shape, dtype, flops):
    return kernel_calls(body, inputs, [jax.ShapeDtypeStruct(shape, dtype)], flops)[0]


def kernel_calls(body, inputs, outputs, flops):
    return pl.pallas_call(
        body,
        out_shape=outputs,
        in_specs=[VMEM] * len(inputs),
        out_specs=[VMEM] * len(outputs),
        cost_estimate=pl.CostEstimate(flops=flops, bytes_accessed=0, transcendentals=0),
        compiler_params=pltpu.CompilerParams(vmem_limit_bytes=40 * 2**20),
    )(*inputs)


def swap(array):
    return lax.ppermute(array, "core", [(0, 1), (1, 0)])


def exchange(array, axes):
    return lax.all_to_all(array, axes, 0, 0, tiled=True)


def stack(blocks):
    return jnp.concatenate([block.reshape(192, 224) for block in blocks], axis=0)


def places():
    for member in range(8):
        bit = {name: member >> (2 - at) & 1 for at, name in enumerate(Z)}
        yield member, bit["z2"] * 2 + bit["z1"], bit["z0"]


def pack_body(momentum, sent, kept):
    for member, layer, h in places():
        sent[member] = momentum[layer, :, h * 224 : h * 224 + 224]
    kept[...] = momentum[...]


def shard_body(both, out):
    for columns in range(2):
        out[columns] = both[columns, pl.ds(lax.axis_index("core") * 4, 4)]


def gram_body(both, m, out):
    for group in range(2):
        total = jnp.zeros((384, 384), F32)
        for columns in range(2):
            total = total + lax.dot_general(
                both[columns].reshape(384, 224),
                stack([m[2 * group + i, columns] for i in range(2)]),
                (((1,), (1,)), ((), ())),
                preferred_element_type=F32,
            )
        out[:, group] = total.astype(BF16).reshape(8, 48, 384)


def send_body(m, out):
    out[...] = m[:, 1 - lax.axis_index("core")]


def times(tiles, groups):
    total = jnp.zeros((384, 224), F32)
    for group in range(2):
        panel = jnp.concatenate([tiles[2 * block + group] for block in range(8)], axis=0)
        total = total + jnp.dot(panel, groups[group], preferred_element_type=F32)
    return total.reshape(8, 48, 224)


def first_body(m, tiles, out):
    core = lax.axis_index("core")
    out[...] = times(tiles, [stack([m[2 * g + i, core] for i in range(2)]) for g in range(2)])


def weight_body(both, got, others, first, out):
    core = lax.axis_index("core")
    theirs = got.at[1 - core]
    groups = [stack([theirs[2 * g + i] for i in range(2)]) for g in range(2)]
    gm = first[...] + times(others, groups)
    out[...] = (A3 * both[core].astype(F32) + A5 * gm).astype(BF16)


def product_body(w, tiles, others, out):
    core = lax.axis_index("core")
    total = jnp.zeros((8, 48, 224), F32)
    for held, h in ((tiles, core), (others, 1 - core)):
        groups = [
            stack([w[2 * g + i, pl.ds(h * 4, 4)] for i in range(2)]) for g in range(2)
        ]
        total = total + times(held, groups)
    out[...] = total.astype(BF16)


def local(momentum):
    width = 7168
    packed = jax.ShapeDtypeStruct((8, 48, 224), BF16)
    kept = jax.ShapeDtypeStruct(momentum.shape, BF16)
    sent, kept = kernel_calls(pack_body, [momentum], [packed, kept], 10**6)
    flops = 2 * 384 * 768 * 224
    both = lax.all_gather(exchange(sent, Z), "core", axis=0)
    shard = kernel_call(shard_body, [both], (2, 4, 48, 224), BF16, 10**6)
    m = lax.all_gather(shard, X, axis=0)
    part = kernel_call(gram_body, [both, m], (8, 2, 48, 384), BF16, 2 * flops)
    parts = exchange(part.reshape(16, 48, 384), HY)
    tile = jnp.sum(parts.astype(F32), axis=0).astype(BF16)
    tile, later = lax.optimization_barrier((tile, m))
    gathered = exchange(jnp.broadcast_to(tile[None], (16, 48, 384)), HY)
    send = kernel_call(send_body, [later], (4, 4, 48, 224), BF16, 10**6)
    got = lax.all_gather(send, "core", axis=0)
    gathered, got = lax.optimization_barrier((gathered, got))

    others = swap(gathered)
    first = kernel_call(first_body, [m, gathered], (8, 48, 224), F32, flops)
    weighted = kernel_call(
        weight_body, [both, got, others, first], (8, 48, 224), BF16, flops
    )
    w = lax.all_gather(weighted, X, axis=0)
    rows = kernel_call(product_body, [w, gathered, others], (8, 48, 224), BF16, 2 * flops)
    back = exchange(rows, Z).astype(F32)
    at = {(layer, h): member for member, layer, h in places()}
    halves = [[back[at[layer, h]] for layer in range(4)] for h in range(2)]
    product = jnp.concatenate([jnp.stack(half) for half in halves], axis=2)
    result = 0.2 * math.sqrt(width) * (A1 * kept.astype(F32) + product)
    return result.astype(BF16)


def solution(mesh):
    split = Mesh(mesh.devices.reshape((2,) * 9), AXES)
    placed = P(None, AXES[:5], AXES[5:])
    return jax.shard_map(local, mesh=split, in_specs=(placed,), out_specs=placed, check_vma=False)
```

```python
import math

import jax
import jax.numpy as jnp
from jax import lax
from jax.experimental import pallas as pl
from jax.experimental.pallas import tpu as pltpu
from jax.sharding import Mesh, PartitionSpec as P

F32 = jnp.float32
BF16 = jnp.bfloat16
A1, A3, A5 = 3.4445, -4.775, 2.0315
SCALE = 0.2 * math.sqrt(7168)
KAPPA = 2.7
Z = ("z0", "z1", "z2")
HY = ("z0", "y2", "y1", "y0")
X = ("x1", "x0")
AXES = ("z2", "z1", "z0", "x1", "x0", "y2", "y1", "y0", "core")
VMEM = pl.BlockSpec(memory_space=pltpu.VMEM)


def kernel_call(body, inputs, shape, dtype, flops):
    return kernel_calls(body, inputs, [jax.ShapeDtypeStruct(shape, dtype)], flops)[0]


def kernel_calls(body, inputs, outputs, flops):
    return pl.pallas_call(
        body,
        out_shape=outputs,
        in_specs=[VMEM] * len(inputs),
        out_specs=[VMEM] * len(outputs),
        cost_estimate=pl.CostEstimate(flops=flops, bytes_accessed=0, transcendentals=0),
        compiler_params=pltpu.CompilerParams(vmem_limit_bytes=40 * 2**20),
    )(*inputs)


def swap(array):
    return lax.ppermute(array, "core", [(0, 1), (1, 0)])


def exchange(array, axes):
    return lax.all_to_all(array, axes, 0, 0, tiled=True)


def stack(blocks):
    return jnp.concatenate([block.reshape(192, 224) for block in blocks], axis=0)


def places():
    for member in range(8):
        bit = {name: member >> (2 - at) & 1 for at, name in enumerate(Z)}
        yield member, bit["z2"] * 2 + bit["z1"], bit["z0"]


def pack_body(momentum, sent):
    for member, layer, h in places():
        sent[member] = momentum[layer, :, h * 224 : h * 224 + 224]


def shard_body(both, out):
    for columns in range(2):
        out[columns] = both[columns, pl.ds(lax.axis_index("core") * 4, 4)]


def gram_body(both, m, out):
    for group in range(2):
        total = jnp.zeros((384, 384), F32)
        for columns in range(2):
            total = total + lax.dot_general(
                both[columns].reshape(384, 224),
                stack([m[2 * group + i, columns] for i in range(2)]),
                (((1,), (1,)), ((), ())),
                preferred_element_type=F32,
            )
        out[:, group] = total.astype(BF16).reshape(8, 48, 384)


def send_body(m, out):
    out[...] = m[:, 1 - lax.axis_index("core")]


def times(tiles, groups):
    total = jnp.zeros((384, 224), F32)
    for group in range(2):
        panel = jnp.concatenate([tiles[2 * block + group] for block in range(8)], axis=0)
        total = total + jnp.dot(panel, groups[group], preferred_element_type=F32)
    return total.reshape(8, 48, 224)


def first_body(m, tiles, out):
    core = lax.axis_index("core")
    out[...] = times(tiles, [stack([m[2 * g + i, core] for i in range(2)]) for g in range(2)])


def weight_body(both, got, others, first, out, product):
    core = lax.axis_index("core")
    theirs = got.at[1 - core]
    groups = [stack([theirs[2 * g + i] for i in range(2)]) for g in range(2)]
    gm = first[...] + times(others, groups)
    out[...] = ((A3 + KAPPA) * both[core].astype(F32) + A5 * gm).astype(BF16)
    product[...] = gm


def product_body(w, tiles, others, both, gm, out):
    core = lax.axis_index("core")
    total = A1 * both[core].astype(F32) - KAPPA * gm[...]
    for held, h in ((tiles, core), (others, 1 - core)):
        groups = [
            stack([w[2 * g + i, pl.ds(h * 4, 4)] for i in range(2)]) for g in range(2)
        ]
        total = total + times(held, groups)
    out[...] = (SCALE * total).astype(BF16)


def local(momentum):
    sent = kernel_call(pack_body, [momentum], (8, 48, 224), BF16, 10**6)
    flops = 2 * 384 * 768 * 224
    both = lax.all_gather(exchange(sent, Z), "core", axis=0)
    shard = kernel_call(shard_body, [both], (2, 4, 48, 224), BF16, 10**6)
    m = lax.all_gather(shard, X, axis=0)
    part = kernel_call(gram_body, [both, m], (8, 2, 48, 384), BF16, 2 * flops)
    parts = exchange(part.reshape(16, 48, 384), HY)
    tile = jnp.sum(parts.astype(F32), axis=0).astype(BF16)
    tile, later = lax.optimization_barrier((tile, m))
    gathered = exchange(jnp.broadcast_to(tile[None], (16, 48, 384)), HY)
    send = kernel_call(send_body, [later], (4, 4, 48, 224), BF16, 10**6)
    got = lax.all_gather(send, "core", axis=0)
    gathered, got = lax.optimization_barrier((gathered, got))

    others = swap(gathered)
    first = kernel_call(first_body, [m, gathered], (8, 48, 224), F32, flops)
    block = (8, 48, 224)
    outputs = [jax.ShapeDtypeStruct(block, BF16), jax.ShapeDtypeStruct(block, F32)]
    weighted, gm = kernel_calls(weight_body, [both, got, others, first], outputs, flops)
    w = lax.all_gather(weighted, X, axis=0)
    rows = kernel_call(
        product_body, [w, gathered, others, both, gm], block, BF16, 2 * flops
    )
    back = exchange(rows, Z)
    at = {(layer, h): member for member, layer, h in places()}
    halves = [[back[at[layer, h]] for layer in range(4)] for h in range(2)]
    return jnp.concatenate([jnp.stack(half) for half in halves], axis=2)


def solution(mesh):
    split = Mesh(mesh.devices.reshape((2,) * 9), AXES)
    placed = P(None, AXES[:5], AXES[5:])
    return jax.shard_map(local, mesh=split, in_specs=(placed,), out_specs=placed, check_vma=False)
```

```python
import math

import jax
import jax.numpy as jnp
from jax import lax
from jax.experimental import pallas as pl
from jax.experimental.pallas import tpu as pltpu
from jax.sharding import Mesh, PartitionSpec as P

F32 = jnp.float32
BF16 = jnp.bfloat16
A1, A3, A5 = 3.4445, -4.775, 2.0315
SCALE = 0.2 * math.sqrt(7168)
KAPPA = 2.7
Z = ("z0", "z1", "z2")
HY = ("z0", "y2", "y1", "y0")
X = ("x1", "x0")
AXES = ("z2", "z1", "z0", "x1", "x0", "y2", "y1", "y0", "core")
VMEM = pl.BlockSpec(memory_space=pltpu.VMEM)


def kernel_call(body, inputs, shape, dtype, flops, scratch=()):
    return kernel_calls(body, inputs, [jax.ShapeDtypeStruct(shape, dtype)], flops, scratch)[0]


def kernel_calls(body, inputs, outputs, flops, scratch=()):
    return pl.pallas_call(
        body,
        out_shape=outputs,
        in_specs=[VMEM] * len(inputs),
        out_specs=[VMEM] * len(outputs),
        scratch_shapes=scratch,
        cost_estimate=pl.CostEstimate(flops=flops, bytes_accessed=0, transcendentals=0),
        compiler_params=pltpu.CompilerParams(vmem_limit_bytes=40 * 2**20),
    )(*inputs)


def swap(array):
    return lax.ppermute(array, "core", [(0, 1), (1, 0)])


def exchange(array, axes):
    return lax.all_to_all(array, axes, 0, 0, tiled=True)


def stack(blocks):
    return jnp.concatenate([block.reshape(192, 224) for block in blocks], axis=0)


def places():
    for member in range(8):
        bit = {name: member >> (2 - at) & 1 for at, name in enumerate(Z)}
        yield member, bit["z2"] * 2 + bit["z1"], bit["z0"]


def pack_body(momentum, sent):
    for member, layer, h in places():
        sent[member] = momentum[layer, :, h * 224 : h * 224 + 224]


def shard_body(both, out):
    for columns in range(2):
        out[columns] = both[columns, pl.ds(lax.axis_index("core") * 4, 4)]


def gram_body(both, m, out):
    for group in range(2):
        total = jnp.zeros((384, 384), F32)
        for columns in range(2):
            total = total + lax.dot_general(
                both[columns].reshape(384, 224),
                stack([m[2 * group + i, columns] for i in range(2)]),
                (((1,), (1,)), ((), ())),
                preferred_element_type=F32,
            )
        out[:, group] = total.astype(BF16).reshape(8, 48, 384)


def send_body(m, out):
    out[...] = m[:, 1 - lax.axis_index("core")]


def times(tiles, groups):
    total = jnp.zeros((384, 224), F32)
    for group in range(2):
        panel = jnp.concatenate([tiles[2 * block + group] for block in range(8)], axis=0)
        total = total + jnp.dot(panel, groups[group], preferred_element_type=F32)
    return total.reshape(8, 48, 224)


def first_body(m, tiles, out):
    core = lax.axis_index("core")
    out[...] = times(tiles, [stack([m[2 * g + i, core] for i in range(2)]) for g in range(2)])


def squeeze(blocks, out):
    for z in range(8):
        out[z] = blocks[z][:, :128]
    for h in range(2):
        tails = jnp.concatenate([blocks[h * 4 + i][:, 128:] for i in range(4)], axis=1)
        for k in range(3):
            out[8 + h * 3 + k] = tails[:, k * 128 : k * 128 + 128]


def unsqueeze(packed, w):
    for x in range(4):
        for h in range(2):
            tails = jnp.concatenate([packed[x, 8 + h * 3 + k] for k in range(3)], axis=1)
            for i in range(4):
                tail = tails[:, i * 96 : i * 96 + 96]
                w[x, h * 4 + i] = jnp.concatenate([packed[x, h * 4 + i], tail], axis=1)


def weight_body(both, got, others, first, out, product):
    core = lax.axis_index("core")
    theirs = got.at[1 - core]
    groups = [stack([theirs[2 * g + i] for i in range(2)]) for g in range(2)]
    gm = first[...] + times(others, groups)
    w = ((A3 + KAPPA) * both[core].astype(F32) + A5 * gm).astype(BF16)
    squeeze([w[z] for z in range(8)], out)
    product[...] = gm


def product_body(packed, tiles, others, both, gm, out, w):
    unsqueeze(packed, w)
    core = lax.axis_index("core")
    total = A1 * both[core].astype(F32) - KAPPA * gm[...]
    for held, h in ((tiles, core), (others, 1 - core)):
        groups = [
            stack([w[2 * g + i, pl.ds(h * 4, 4)] for i in range(2)]) for g in range(2)
        ]
        total = total + times(held, groups)
    out[...] = (SCALE * total).astype(BF16)


def local(momentum):
    sent = kernel_call(pack_body, [momentum], (8, 48, 224), BF16, 10**6)
    flops = 2 * 384 * 768 * 224
    both = lax.all_gather(exchange(sent, Z), "core", axis=0)
    shard = kernel_call(shard_body, [both], (2, 4, 48, 224), BF16, 10**6)
    m = lax.all_gather(shard, X, axis=0)
    part = kernel_call(gram_body, [both, m], (8, 2, 48, 384), BF16, 2 * flops)
    parts = exchange(part.reshape(16, 48, 384), HY)
    tile = jnp.sum(parts.astype(F32), axis=0).astype(BF16)
    tile, later = lax.optimization_barrier((tile, m))
    gathered = exchange(jnp.broadcast_to(tile[None], (16, 48, 384)), HY)
    send = kernel_call(send_body, [later], (4, 4, 48, 224), BF16, 10**6)
    got = lax.all_gather(send, "core", axis=0)
    gathered, got = lax.optimization_barrier((gathered, got))

    others = swap(gathered)
    first = kernel_call(first_body, [m, gathered], (8, 48, 224), F32, flops)
    block = (8, 48, 224)
    outputs = [jax.ShapeDtypeStruct((14, 48, 128), BF16), jax.ShapeDtypeStruct(block, F32)]
    weighted, gm = kernel_calls(weight_body, [both, got, others, first], outputs, flops)
    w = lax.all_gather(weighted, X, axis=0)
    rows = kernel_call(
        product_body,
        [w, gathered, others, both, gm],
        block,
        BF16,
        2 * flops,
        [pltpu.VMEM((4, 8, 48, 224), BF16)],
    )
    back = exchange(rows, Z)
    at = {(layer, h): member for member, layer, h in places()}
    halves = [[back[at[layer, h]] for layer in range(4)] for h in range(2)]
    return jnp.concatenate([jnp.stack(half) for half in halves], axis=2)


def solution(mesh):
    split = Mesh(mesh.devices.reshape((2,) * 9), AXES)
    placed = P(None, AXES[:5], AXES[5:])
    return jax.shard_map(local, mesh=split, in_specs=(placed,), out_specs=placed, check_vma=False)
```

```python
import math

import jax
import jax.numpy as jnp
from jax import lax
from jax.experimental import pallas as pl
from jax.experimental.pallas import tpu as pltpu
from jax.sharding import Mesh, PartitionSpec as P

F32 = jnp.float32
BF16 = jnp.bfloat16
A1, A3, A5 = 3.4445, -4.775, 2.0315
SCALE = 0.2 * math.sqrt(7168)
KAPPA = 2.7
Z = ("z0", "z1", "z2")
HY = ("z0", "y2", "y1", "y0")
X = ("x1", "x0")
AXES = ("z2", "z1", "z0", "x1", "x0", "y2", "y1", "y0", "core")
VMEM = pl.BlockSpec(memory_space=pltpu.VMEM)


def kernel_call(body, inputs, shape, dtype, flops, scratch=()):
    return kernel_calls(body, inputs, [jax.ShapeDtypeStruct(shape, dtype)], flops, scratch)[0]


def kernel_calls(body, inputs, outputs, flops, scratch=()):
    return pl.pallas_call(
        body,
        out_shape=outputs,
        in_specs=[VMEM] * len(inputs),
        out_specs=[VMEM] * len(outputs),
        scratch_shapes=scratch,
        cost_estimate=pl.CostEstimate(flops=flops, bytes_accessed=0, transcendentals=0),
        compiler_params=pltpu.CompilerParams(vmem_limit_bytes=40 * 2**20),
    )(*inputs)


def swap(array):
    return lax.ppermute(array, "core", [(0, 1), (1, 0)])


def exchange(array, axes):
    return lax.all_to_all(array, axes, 0, 0, tiled=True)


def stack(blocks):
    return jnp.concatenate([block.reshape(192, 224) for block in blocks], axis=0)


def places():
    for member in range(8):
        bit = {name: member >> (2 - at) & 1 for at, name in enumerate(Z)}
        yield member, bit["z2"] * 2 + bit["z1"], bit["z0"]


def pack_body(momentum, sent):
    for member, layer, h in places():
        sent[member] = momentum[layer, :, h * 224 : h * 224 + 224]


def squeeze(blocks, out):
    for z in range(8):
        out[z] = blocks[z][:, :128]
    for h in range(2):
        tails = jnp.concatenate([blocks[h * 4 + i][:, 128:] for i in range(4)], axis=1)
        for k in range(3):
            out[8 + h * 3 + k] = tails[:, k * 128 : k * 128 + 128]


def unsqueeze(packed, w):
    for x in range(4):
        for h in range(2):
            tails = jnp.concatenate([packed[x, 8 + h * 3 + k] for k in range(3)], axis=1)
            for i in range(4):
                tail = tails[:, i * 96 : i * 96 + 96]
                w[x, h * 4 + i] = jnp.concatenate([packed[x, h * 4 + i], tail], axis=1)


def shard_body(both, out):
    mine = pl.ds(lax.axis_index("core") * 4, 4)
    blocks = [both[columns, mine] for columns in range(2)]
    squeeze([blocks[k // 4][k % 4] for k in range(8)], out)


def gram_body(both, packed, out, m):
    unsqueeze(packed, m)
    for group in range(2):
        total = jnp.zeros((384, 384), F32)
        for columns in range(2):
            total = total + lax.dot_general(
                both[columns].reshape(384, 224),
                stack([m[2 * group + i, columns * 4 : columns * 4 + 4] for i in range(2)]),
                (((1,), (1,)), ((), ())),
                preferred_element_type=F32,
            )
        out[:, group] = total.astype(BF16).reshape(8, 48, 384)


def send_body(m, out):
    out[...] = m[:, pl.ds((1 - lax.axis_index("core")) * 4, 4)]


def times(tiles, groups):
    total = jnp.zeros((384, 224), F32)
    for group in range(2):
        panel = jnp.concatenate([tiles[2 * block + group] for block in range(8)], axis=0)
        total = total + jnp.dot(panel, groups[group], preferred_element_type=F32)
    return total.reshape(8, 48, 224)


def first_body(m, tiles, out):
    own = pl.ds(lax.axis_index("core") * 4, 4)
    out[...] = times(tiles, [stack([m[2 * g + i, own] for i in range(2)]) for g in range(2)])


def weight_body(both, got, others, first, out, product):
    core = lax.axis_index("core")
    theirs = got.at[1 - core]
    groups = [stack([theirs[2 * g + i] for i in range(2)]) for g in range(2)]
    gm = first[...] + times(others, groups)
    w = ((A3 + KAPPA) * both[core].astype(F32) + A5 * gm).astype(BF16)
    squeeze([w[z] for z in range(8)], out)
    product[...] = gm


def product_body(packed, tiles, others, both, gm, out, w):
    unsqueeze(packed, w)
    core = lax.axis_index("core")
    total = A1 * both[core].astype(F32) - KAPPA * gm[...]
    for held, h in ((tiles, core), (others, 1 - core)):
        groups = [
            stack([w[2 * g + i, pl.ds(h * 4, 4)] for i in range(2)]) for g in range(2)
        ]
        total = total + times(held, groups)
    out[...] = (SCALE * total).astype(BF16)


def local(momentum):
    sent = kernel_call(pack_body, [momentum], (8, 48, 224), BF16, 10**6)
    flops = 2 * 384 * 768 * 224
    both = lax.all_gather(exchange(sent, Z), "core", axis=0)
    shard = kernel_call(shard_body, [both], (14, 48, 128), BF16, 10**6)
    outputs = [jax.ShapeDtypeStruct(dims, BF16) for dims in ((8, 2, 48, 384), (4, 8, 48, 224))]
    packed = lax.all_gather(shard, X, axis=0)
    part, m = kernel_calls(gram_body, [both, packed], outputs, 2 * flops)
    parts = exchange(part.reshape(16, 48, 384), HY)
    tile = jnp.sum(parts.astype(F32), axis=0).astype(BF16)
    tile, later = lax.optimization_barrier((tile, m))
    gathered = exchange(jnp.broadcast_to(tile[None], (16, 48, 384)), HY)
    send = kernel_call(send_body, [later], (4, 4, 48, 224), BF16, 10**6)
    got = lax.all_gather(send, "core", axis=0)
    gathered, got = lax.optimization_barrier((gathered, got))

    others = swap(gathered)
    first = kernel_call(first_body, [m, gathered], (8, 48, 224), F32, flops)
    block = (8, 48, 224)
    outputs = [jax.ShapeDtypeStruct((14, 48, 128), BF16), jax.ShapeDtypeStruct(block, F32)]
    weighted, gm = kernel_calls(weight_body, [both, got, others, first], outputs, flops)
    w = lax.all_gather(weighted, X, axis=0)
    rows = kernel_call(
        product_body,
        [w, gathered, others, both, gm],
        block,
        BF16,
        2 * flops,
        [pltpu.VMEM((4, 8, 48, 224), BF16)],
    )
    back = exchange(rows, Z)
    at = {(layer, h): member for member, layer, h in places()}
    halves = [[back[at[layer, h]] for layer in range(4)] for h in range(2)]
    return jnp.concatenate([jnp.stack(half) for half in halves], axis=2)


def solution(mesh):
    split = Mesh(mesh.devices.reshape((2,) * 9), AXES)
    placed = P(None, AXES[:5], AXES[5:])
    return jax.shard_map(local, mesh=split, in_specs=(placed,), out_specs=placed, check_vma=False)
```

```python
import math

import jax
import jax.numpy as jnp
from jax import lax
from jax.experimental import pallas as pl
from jax.experimental.pallas import tpu as pltpu
from jax.sharding import Mesh, PartitionSpec as P

F32 = jnp.float32
BF16 = jnp.bfloat16
A1, A3, A5 = 3.4445, -4.775, 2.0315
SCALE = 0.2 * math.sqrt(7168)
KAPPA = 2.7
Z = ("z0", "z1", "z2")
HY = ("z0", "y2", "y1", "y0")
X = ("x1", "x0")
AXES = ("z2", "z1", "z0", "x1", "x0", "y2", "y1", "y0", "core")
VMEM = pl.BlockSpec(memory_space=pltpu.VMEM)


def kernel_call(body, inputs, shape, dtype, flops, scratch=()):
    return kernel_calls(body, inputs, [jax.ShapeDtypeStruct(shape, dtype)], flops, scratch)[0]


def kernel_calls(body, inputs, outputs, flops, scratch=()):
    return pl.pallas_call(
        body,
        out_shape=outputs,
        in_specs=[VMEM] * len(inputs),
        out_specs=[VMEM] * len(outputs),
        scratch_shapes=scratch,
        cost_estimate=pl.CostEstimate(flops=flops, bytes_accessed=0, transcendentals=0),
        compiler_params=pltpu.CompilerParams(vmem_limit_bytes=40 * 2**20),
    )(*inputs)


def swap(array):
    return lax.ppermute(array, "core", [(0, 1), (1, 0)])


def exchange(array, axes):
    return lax.all_to_all(array, axes, 0, 0, tiled=True)


def stack(blocks):
    return jnp.concatenate([block.reshape(192, 224) for block in blocks], axis=0)


def places():
    for member in range(8):
        bit = {name: member >> (2 - at) & 1 for at, name in enumerate(Z)}
        yield member, bit["z2"] * 2 + bit["z1"], bit["z0"]


def pack_body(momentum, sent):
    for member, layer, h in places():
        sent[member] = momentum[layer, :, h * 224 : h * 224 + 224]


def squeeze(blocks, out):
    for z in range(8):
        out[z] = blocks[z][:, :128]
    for h in range(2):
        last = blocks[h * 4 + 3][:, 128:]
        for k in range(3):
            third = last[:, k * 32 : k * 32 + 32]
            out[8 + h * 3 + k] = jnp.concatenate([blocks[h * 4 + k][:, 128:], third], axis=1)


def unsqueeze(packed, w):
    for x in range(4):
        for h in range(2):
            tiles = [packed[x, 8 + h * 3 + k] for k in range(3)]
            tails = [tile[:, :96] for tile in tiles]
            tails.append(jnp.concatenate([tile[:, 96:] for tile in tiles], axis=1))
            for i in range(4):
                w[x, h * 4 + i] = jnp.concatenate([packed[x, h * 4 + i], tails[i]], axis=1)


def shard_body(both, out):
    mine = pl.ds(lax.axis_index("core") * 4, 4)
    blocks = [both[columns, mine] for columns in range(2)]
    squeeze([blocks[k // 4][k % 4] for k in range(8)], out)


def gram_body(both, packed, out, m):
    unsqueeze(packed, m)
    for group in range(2):
        total = jnp.zeros((384, 384), F32)
        for columns in range(2):
            total = total + lax.dot_general(
                both[columns].reshape(384, 224),
                stack([m[2 * group + i, columns * 4 : columns * 4 + 4] for i in range(2)]),
                (((1,), (1,)), ((), ())),
                preferred_element_type=F32,
            )
        out[:, group] = total.astype(BF16).reshape(8, 48, 384)


def send_body(m, out):
    out[...] = m[:, pl.ds((1 - lax.axis_index("core")) * 4, 4)]


def times(tiles, groups):
    total = jnp.zeros((384, 224), F32)
    for group in range(2):
        panel = jnp.concatenate([tiles[2 * block + group] for block in range(8)], axis=0)
        total = total + jnp.dot(panel, groups[group], preferred_element_type=F32)
    return total.reshape(8, 48, 224)


def first_body(m, tiles, out):
    own = pl.ds(lax.axis_index("core") * 4, 4)
    out[...] = times(tiles, [stack([m[2 * g + i, own] for i in range(2)]) for g in range(2)])


def weight_body(both, got, others, first, out, product):
    core = lax.axis_index("core")
    theirs = got.at[1 - core]
    groups = [stack([theirs[2 * g + i] for i in range(2)]) for g in range(2)]
    gm = first[...] + times(others, groups)
    w = ((A3 + KAPPA) * both[core].astype(F32) + A5 * gm).astype(BF16)
    squeeze([w[z] for z in range(8)], out)
    product[...] = gm


def product_body(packed, tiles, others, both, gm, out, w):
    unsqueeze(packed, w)
    core = lax.axis_index("core")
    total = A1 * both[core].astype(F32) - KAPPA * gm[...]
    for held, h in ((tiles, core), (others, 1 - core)):
        groups = [
            stack([w[2 * g + i, pl.ds(h * 4, 4)] for i in range(2)]) for g in range(2)
        ]
        total = total + times(held, groups)
    out[...] = (SCALE * total).astype(BF16)


def local(momentum):
    sent = kernel_call(pack_body, [momentum], (8, 48, 224), BF16, 10**6)
    flops = 2 * 384 * 768 * 224
    both = lax.all_gather(exchange(sent, Z), "core", axis=0)
    shard = kernel_call(shard_body, [both], (14, 48, 128), BF16, 10**6)
    outputs = [jax.ShapeDtypeStruct(dims, BF16) for dims in ((8, 2, 48, 384), (4, 8, 48, 224))]
    packed = lax.all_gather(shard, X, axis=0)
    part, m = kernel_calls(gram_body, [both, packed], outputs, 2 * flops)
    parts = exchange(part.reshape(16, 48, 384), HY)
    tile = jnp.sum(parts.astype(F32), axis=0).astype(BF16)
    tile, later = lax.optimization_barrier((tile, m))
    gathered = exchange(jnp.broadcast_to(tile[None], (16, 48, 384)), HY)
    send = kernel_call(send_body, [later], (4, 4, 48, 224), BF16, 10**6)
    got = lax.all_gather(send, "core", axis=0)
    gathered, got = lax.optimization_barrier((gathered, got))

    others = swap(gathered)
    first = kernel_call(first_body, [m, gathered], (8, 48, 224), F32, flops)
    block = (8, 48, 224)
    outputs = [jax.ShapeDtypeStruct((14, 48, 128), BF16), jax.ShapeDtypeStruct(block, F32)]
    weighted, gm = kernel_calls(weight_body, [both, got, others, first], outputs, flops)
    w = lax.all_gather(weighted, X, axis=0)
    rows = kernel_call(
        product_body,
        [w, gathered, others, both, gm],
        block,
        BF16,
        2 * flops,
        [pltpu.VMEM((4, 8, 48, 224), BF16)],
    )
    back = exchange(rows, Z)
    at = {(layer, h): member for member, layer, h in places()}
    halves = [[back[at[layer, h]] for layer in range(4)] for h in range(2)]
    return jnp.concatenate([jnp.stack(half) for half in halves], axis=2)


def solution(mesh):
    split = Mesh(mesh.devices.reshape((2,) * 9), AXES)
    placed = P(None, AXES[:5], AXES[5:])
    return jax.shard_map(local, mesh=split, in_specs=(placed,), out_specs=placed, check_vma=False)
```

```python
import math

import jax
import jax.numpy as jnp
from jax import lax
from jax.experimental import pallas as pl
from jax.experimental.pallas import tpu as pltpu
from jax.sharding import Mesh, PartitionSpec as P

F32 = jnp.float32
BF16 = jnp.bfloat16
A1, A3, A5 = 3.4445, -4.775, 2.0315
SCALE = 0.2 * math.sqrt(7168)
KAPPA = 2.7
Z = ("z1", "z0", "z2")
HY = ("z0", "y2", "y1", "y0")
X = ("x1", "x0")
AXES = ("z2", "z1", "z0", "x1", "x0", "y2", "y1", "y0", "core")
VMEM = pl.BlockSpec(memory_space=pltpu.VMEM)


def kernel_call(body, inputs, shape, dtype, flops, scratch=()):
    return kernel_calls(body, inputs, [jax.ShapeDtypeStruct(shape, dtype)], flops, scratch)[0]


def kernel_calls(body, inputs, outputs, flops, scratch=()):
    return pl.pallas_call(
        body,
        out_shape=outputs,
        in_specs=[VMEM] * len(inputs),
        out_specs=[VMEM] * len(outputs),
        scratch_shapes=scratch,
        cost_estimate=pl.CostEstimate(flops=flops, bytes_accessed=0, transcendentals=0),
        compiler_params=pltpu.CompilerParams(vmem_limit_bytes=40 * 2**20),
    )(*inputs)


def swap(array):
    return lax.ppermute(array, "core", [(0, 1), (1, 0)])


def exchange(array, axes):
    return lax.all_to_all(array, axes, 0, 0, tiled=True)


def stack(blocks):
    return jnp.concatenate([block.reshape(192, 224) for block in blocks], axis=0)


def places():
    for member in range(8):
        bit = {name: member >> (2 - at) & 1 for at, name in enumerate(Z)}
        yield member, bit["z2"] * 2 + bit["z1"], bit["z0"]


def pack_body(momentum, sent):
    for member, layer, h in places():
        sent[member] = momentum[layer, :, h * 224 : h * 224 + 224]


def squeeze(blocks, out):
    for z in range(8):
        out[z] = blocks[z][:, :128]
    for h in range(2):
        last = blocks[h * 4 + 3][:, 128:]
        for k in range(3):
            third = last[:, k * 32 : k * 32 + 32]
            out[8 + h * 3 + k] = jnp.concatenate([blocks[h * 4 + k][:, 128:], third], axis=1)


def unsqueeze(packed, w):
    for x in range(4):
        for h in range(2):
            tiles = [packed[x, 8 + h * 3 + k] for k in range(3)]
            tails = [tile[:, :96] for tile in tiles]
            tails.append(jnp.concatenate([tile[:, 96:] for tile in tiles], axis=1))
            for i in range(4):
                w[x, h * 4 + i] = jnp.concatenate([packed[x, h * 4 + i], tails[i]], axis=1)


def shard_body(both, out):
    mine = pl.ds(lax.axis_index("core") * 4, 4)
    blocks = [both[columns, mine] for columns in range(2)]
    squeeze([blocks[k // 4][k % 4] for k in range(8)], out)


def gram_body(both, packed, out, m):
    unsqueeze(packed, m)
    for group in range(2):
        total = jnp.zeros((384, 384), F32)
        for columns in range(2):
            total = total + lax.dot_general(
                both[columns].reshape(384, 224),
                stack([m[2 * group + i, columns * 4 : columns * 4 + 4] for i in range(2)]),
                (((1,), (1,)), ((), ())),
                preferred_element_type=F32,
            )
        out[:, group] = total.astype(BF16).reshape(8, 48, 384)


def send_body(m, out):
    out[...] = m[:, pl.ds((1 - lax.axis_index("core")) * 4, 4)]


def times(tiles, groups):
    total = jnp.zeros((384, 224), F32)
    for group in range(2):
        panel = jnp.concatenate([tiles[2 * block + group] for block in range(8)], axis=0)
        total = total + jnp.dot(panel, groups[group], preferred_element_type=F32)
    return total.reshape(8, 48, 224)


def first_body(m, tiles, out):
    own = pl.ds(lax.axis_index("core") * 4, 4)
    out[...] = times(tiles, [stack([m[2 * g + i, own] for i in range(2)]) for g in range(2)])


def weight_body(both, got, others, first, out, product):
    core = lax.axis_index("core")
    theirs = got.at[1 - core]
    groups = [stack([theirs[2 * g + i] for i in range(2)]) for g in range(2)]
    gm = first[...] + times(others, groups)
    w = ((A3 + KAPPA) * both[core].astype(F32) + A5 * gm).astype(BF16)
    squeeze([w[z] for z in range(8)], out)
    product[...] = gm


def product_body(packed, tiles, others, both, gm, out, w):
    unsqueeze(packed, w)
    core = lax.axis_index("core")
    total = A1 * both[core].astype(F32) - KAPPA * gm[...]
    for held, h in ((tiles, core), (others, 1 - core)):
        groups = [
            stack([w[2 * g + i, pl.ds(h * 4, 4)] for i in range(2)]) for g in range(2)
        ]
        total = total + times(held, groups)
    out[...] = (SCALE * total).astype(BF16)


def local(momentum):
    sent = kernel_call(pack_body, [momentum], (8, 48, 224), BF16, 10**6)
    flops = 2 * 384 * 768 * 224
    both = lax.all_gather(exchange(sent, Z), "core", axis=0)
    shard = kernel_call(shard_body, [both], (14, 48, 128), BF16, 10**6)
    outputs = [jax.ShapeDtypeStruct(dims, BF16) for dims in ((8, 2, 48, 384), (4, 8, 48, 224))]
    packed = lax.all_gather(shard, X, axis=0)
    part, m = kernel_calls(gram_body, [both, packed], outputs, 2 * flops)
    parts = exchange(part.reshape(16, 48, 384), HY)
    tile = jnp.sum(parts.astype(F32), axis=0).astype(BF16)
    tile, later = lax.optimization_barrier((tile, m))
    gathered = exchange(jnp.broadcast_to(tile[None], (16, 48, 384)), HY)
    send = kernel_call(send_body, [later], (4, 4, 48, 224), BF16, 10**6)
    got = lax.all_gather(send, "core", axis=0)
    gathered, got = lax.optimization_barrier((gathered, got))

    others = swap(gathered)
    first = kernel_call(first_body, [m, gathered], (8, 48, 224), F32, flops)
    block = (8, 48, 224)
    outputs = [jax.ShapeDtypeStruct((14, 48, 128), BF16), jax.ShapeDtypeStruct(block, F32)]
    weighted, gm = kernel_calls(weight_body, [both, got, others, first], outputs, flops)
    w = lax.all_gather(weighted, X, axis=0)
    rows = kernel_call(
        product_body,
        [w, gathered, others, both, gm],
        block,
        BF16,
        2 * flops,
        [pltpu.VMEM((4, 8, 48, 224), BF16)],
    )
    back = exchange(rows, Z)
    at = {(layer, h): member for member, layer, h in places()}
    halves = [[back[at[layer, h]] for layer in range(4)] for h in range(2)]
    return jnp.concatenate([jnp.stack(half) for half in halves], axis=2)


def solution(mesh):
    split = Mesh(mesh.devices.reshape((2,) * 9), AXES)
    placed = P(None, AXES[:5], AXES[5:])
    return jax.shard_map(local, mesh=split, in_specs=(placed,), out_specs=placed, check_vma=False)
```

```python
import math

import jax
import jax.numpy as jnp
from jax import lax
from jax.experimental import pallas as pl
from jax.experimental.pallas import tpu as pltpu
from jax.sharding import Mesh, PartitionSpec as P

F32 = jnp.float32
BF16 = jnp.bfloat16
A1, A3, A5 = 3.4445, -4.775, 2.0315
SCALE = 0.2 * math.sqrt(7168)
KAPPA = 2.7
RATIO = KAPPA / A5
Z = ("z0", "z1", "z2")
HY = ("z0", "y2", "y1", "y0")
X = ("x1", "x0")
AXES = ("z2", "z1", "z0", "x1", "x0", "y2", "y1", "y0", "core")
VMEM = pl.BlockSpec(memory_space=pltpu.VMEM)


def kernel_call(body, inputs, shape, dtype, flops, scratch=()):
    return kernel_calls(body, inputs, [jax.ShapeDtypeStruct(shape, dtype)], flops, scratch)[0]


def kernel_calls(body, inputs, outputs, flops, scratch=()):
    return pl.pallas_call(
        body,
        out_shape=outputs,
        in_specs=[VMEM] * len(inputs),
        out_specs=[VMEM] * len(outputs),
        scratch_shapes=scratch,
        cost_estimate=pl.CostEstimate(flops=flops, bytes_accessed=0, transcendentals=0),
        compiler_params=pltpu.CompilerParams(vmem_limit_bytes=40 * 2**20),
    )(*inputs)


def swap(array):
    return lax.ppermute(array, "core", [(0, 1), (1, 0)])


def exchange(array, axes):
    return lax.all_to_all(array, axes, 0, 0, tiled=True)


def stack(blocks):
    return jnp.concatenate([block.reshape(192, 224) for block in blocks], axis=0)


def places():
    for member in range(8):
        bit = {name: member >> (2 - at) & 1 for at, name in enumerate(Z)}
        yield member, bit["z2"] * 2 + bit["z1"], bit["z0"]


def pack_body(momentum, sent):
    for member, layer, h in places():
        sent[member] = momentum[layer, :, h * 224 : h * 224 + 224]


def squeeze(blocks, out):
    for z in range(8):
        out[z] = blocks[z][:, :128]
    for h in range(2):
        last = blocks[h * 4 + 3][:, 128:]
        for k in range(3):
            third = last[:, k * 32 : k * 32 + 32]
            out[8 + h * 3 + k] = jnp.concatenate([blocks[h * 4 + k][:, 128:], third], axis=1)


def unsqueeze(packed, w):
    for x in range(4):
        for h in range(2):
            tiles = [packed[x, 8 + h * 3 + k] for k in range(3)]
            tails = [tile[:, :96] for tile in tiles]
            tails.append(jnp.concatenate([tile[:, 96:] for tile in tiles], axis=1))
            for i in range(4):
                w[x, h * 4 + i] = jnp.concatenate([packed[x, h * 4 + i], tails[i]], axis=1)


def shard_body(both, out):
    mine = pl.ds(lax.axis_index("core") * 4, 4)
    blocks = [both[columns, mine] for columns in range(2)]
    squeeze([blocks[k // 4][k % 4] for k in range(8)], out)


def gram_body(both, packed, out, m):
    unsqueeze(packed, m)
    for group in range(2):
        total = jnp.zeros((384, 384), F32)
        for columns in range(2):
            total = total + lax.dot_general(
                both[columns].reshape(384, 224),
                stack([m[2 * group + i, columns * 4 : columns * 4 + 4] for i in range(2)]),
                (((1,), (1,)), ((), ())),
                preferred_element_type=F32,
            )
        out[:, group] = total.astype(BF16).reshape(8, 48, 384)


def send_body(m, out):
    out[...] = m[:, pl.ds((1 - lax.axis_index("core")) * 4, 4)]


def times(tiles, groups):
    total = jnp.zeros((384, 224), F32)
    for group in range(2):
        panel = jnp.concatenate([tiles[2 * block + group] for block in range(8)], axis=0)
        total = total + jnp.dot(panel, groups[group], preferred_element_type=F32)
    return total.reshape(8, 48, 224)


def first_body(both, m, tiles, out):
    core = lax.axis_index("core")
    own = pl.ds(core * 4, 4)
    gm = times(tiles, [stack([m[2 * g + i, own] for i in range(2)]) for g in range(2)])
    out[...] = (A3 + KAPPA) * both[core].astype(F32) + A5 * gm


def weight_body(got, others, first, out, exact):
    theirs = got.at[1 - lax.axis_index("core")]
    groups = [stack([theirs[2 * g + i] for i in range(2)]) for g in range(2)]
    total = first[...] + A5 * times(others, groups)
    w = total.astype(BF16)
    squeeze([w[z] for z in range(8)], out)
    exact[...] = total


def product_body(packed, tiles, others, both, exact, out, w):
    unsqueeze(packed, w)
    core = lax.axis_index("core")
    total = (A1 + RATIO * (A3 + KAPPA)) * both[core].astype(F32) - RATIO * exact[...]
    for held, h in ((tiles, core), (others, 1 - core)):
        groups = [
            stack([w[2 * g + i, pl.ds(h * 4, 4)] for i in range(2)]) for g in range(2)
        ]
        total = total + times(held, groups)
    out[...] = (SCALE * total).astype(BF16)


def local(momentum):
    sent = kernel_call(pack_body, [momentum], (8, 48, 224), BF16, 10**6)
    flops = 2 * 384 * 768 * 224
    both = lax.all_gather(exchange(sent, Z), "core", axis=0)
    shard = kernel_call(shard_body, [both], (14, 48, 128), BF16, 10**6)
    outputs = [jax.ShapeDtypeStruct(dims, BF16) for dims in ((8, 2, 48, 384), (4, 8, 48, 224))]
    packed = lax.all_gather(shard, X, axis=0)
    part, m = kernel_calls(gram_body, [both, packed], outputs, 2 * flops)
    parts = exchange(part.reshape(16, 48, 384), HY)
    tile = jnp.sum(parts.astype(F32), axis=0).astype(BF16)
    tile, later = lax.optimization_barrier((tile, m))
    gathered = exchange(jnp.broadcast_to(tile[None], (16, 48, 384)), HY)
    send = kernel_call(send_body, [later], (4, 4, 48, 224), BF16, 10**6)
    got = lax.all_gather(send, "core", axis=0)
    gathered, got = lax.optimization_barrier((gathered, got))

    others = swap(gathered)
    first = kernel_call(first_body, [both, m, gathered], (8, 48, 224), F32, flops)
    block = (8, 48, 224)
    outputs = [jax.ShapeDtypeStruct((14, 48, 128), BF16), jax.ShapeDtypeStruct(block, F32)]
    weighted, exact = kernel_calls(weight_body, [got, others, first], outputs, flops)
    w = lax.all_gather(weighted, X, axis=0)
    rows = kernel_call(
        product_body,
        [w, gathered, others, both, exact],
        block,
        BF16,
        2 * flops,
        [pltpu.VMEM((4, 8, 48, 224), BF16)],
    )
    back = exchange(rows, Z)
    at = {(layer, h): member for member, layer, h in places()}
    halves = [[back[at[layer, h]] for layer in range(4)] for h in range(2)]
    return jnp.concatenate([jnp.stack(half) for half in halves], axis=2)


def solution(mesh):
    split = Mesh(mesh.devices.reshape((2,) * 9), AXES)
    placed = P(None, AXES[:5], AXES[5:])
    return jax.shard_map(local, mesh=split, in_specs=(placed,), out_specs=placed, check_vma=False)
```
